256 devices in a mesh: lat: 32 (over z, y_hi, core), lon: 8 (over y_lo, x).
Axes of the slice: x: 4, y: 4 (y_hi: 2, y_lo: 2; y = y_hi * 2 + y_lo), z: 8, core: 2. Of those that a mesh axis runs over, the one named last changes fastest.
Arguments:
- u_wind: float32 [24, 1024, 3072], P(None, 'lat', 'lon'), may hold values from -4 to 4
- v_wind: float32 [24, 1024, 3072], P(None, 'lat', 'lon'), may hold values from -4 to 4
- thickness: float32 [24, 1024, 3072], P(None, 'lat', 'lon'), may hold values from 0.5 to 1.5
- theta: float32 [24, 1024, 3072], P(None, 'lat', 'lon'), may hold values from 0.5 to 1.5
- polar_rows: int32 [32, 16], replicated, may hold values from 0 to 1023, as said below
- cutoffs: int32 [1024], replicated, may hold values from 1 to 768, as said below
Outputs:
- u_next: float32 [24, 1024, 3072], P(None, 'lat', 'lon')
- v_next: float32 [24, 1024, 3072], P(None, 'lat', 'lon')
- thickness_next: float32 [24, 1024, 3072], P(None, 'lat', 'lon')
- heat_next: float32 [24, 1024, 3072], P(None, 'lat', 'lon')
The draws below stay inside these ranges and needn't reach their ends.
Inputs may be any that keep to these rules, and one draw needn't show every extreme that they name: `polar_rows`: each helper lists exactly 16 distinct rows, no row is listed twice, and no helper lists more than 1 row of one index of lat. The listed rows are all rows below a southern edge s and all rows from 1024 - (512 - s) up, with s within 16 of 256. `cutoffs`: the cutoff of row j lies between half of and all of (2 d + 1) * 3072 // 4096 + 1, d = min(j, 1023 - j).
All inputs are finite; a program needn't handle non-finite values.
Results may differ from the reference program's by a relative error of at most 0.0002.
Values sent between devices are 32-bit elements; how exact they have to be, the bound alone decides.
No kernel may reach another device: no remote copies, remote signals or barrier semaphores. Data moves between devices by JAX's collectives and lax.ppermute only.
A program may use at most 128 MiB of HBM per device.

```python
import math
import jax
import jax.numpy as jnp
from jax import lax

NLON = 3072
LEV = 24
LAT_DEV = 32
NLAT = 1024
HROWS = 16


def draw_polar_rows(key, part):
    key = jax.random.fold_in(key, 11)
    shift_key, perm_key = jax.random.split(key)
    lat_count = NLAT // LAT_DEV
    half = NLAT // 2
    south = NLAT // 4 + jax.random.randint(shift_key, (), -(LAT_DEV // 2), LAT_DEV // 2 + 1)
    position = jnp.arange(half)
    row = jnp.where(position < south, position, NLAT - half + position).astype(jnp.int32)
    helper = jax.random.permutation(perm_key, lat_count)
    table = jnp.zeros((lat_count, HROWS), jnp.int32)
    return table.at[helper[position % lat_count], position // lat_count].set(row)


def draw_cutoffs(key, part):
    key = jax.random.fold_in(key, 23)
    row = jnp.arange(NLAT)
    dist = jnp.minimum(row, NLAT - 1 - row)
    high = (2 * dist + 1) * NLON // (4 * NLAT) + 1
    drop = jax.random.randint(key, (NLAT,), 0, high // 2 + 1)
    drop = jnp.where(dist == 0, high // 2, drop)
    drop = jnp.where(dist == NLAT // 2 - 1, 0, drop)
    return (high - drop).astype(jnp.int32)


def level_of(key, extent, cuts, least, largest):
    def one(dim, parts):
        heights = jax.random.uniform(jax.random.fold_in(jax.random.fold_in(key, 6), dim), (parts,), jnp.float32, least / len(cuts), largest / len(cuts))
        return jnp.repeat(jnp.exp(heights), extent[dim] // parts).reshape((-1,) + (1,) * (len(extent) - dim - 1))

    loudness = one(*cuts[0])
    for cut in cuts[1:]:
        loudness = loudness * one(*cut)
    return loudness


def normal_values(rng, extent, spread, reach, cuts=(), kind=jnp.bfloat16):
    values = spread * jax.random.normal(rng, extent, jnp.float32)
    if cuts:
        values = values * level_of(rng, extent, cuts, -0.22, 0.18)
    return jnp.clip(values, -reach, reach).astype(kind)


def setup_inputs(seed: int = 0) -> dict:
    keys = jax.random.split(jax.random.key(seed), 7)
    return {
        "u_wind": normal_values(keys[0], (LEV, NLAT, NLON), 1.0, 4.0, ((1, 32), (2, 8)), jnp.float32),
        "v_wind": normal_values(keys[1], (LEV, NLAT, NLON), 1.0, 4.0, ((1, 32), (2, 8)), jnp.float32),
        "thickness": jnp.clip(0.5 + 1.0 * jax.random.uniform(keys[2], (LEV, NLAT, NLON), jnp.float32) ** level_of(keys[2], (LEV, NLAT, NLON), ((1, 32), (2, 8)), -0.2, 0.2), 0.5, 1.5),
        "theta": jnp.clip(0.5 + 1.0 * jax.random.uniform(keys[3], (LEV, NLAT, NLON), jnp.float32) ** level_of(keys[3], (LEV, NLAT, NLON), ((1, 32), (2, 8)), -0.2, 0.2), 0.5, 1.5),
        "polar_rows": draw_polar_rows(jax.random.fold_in(keys[6], 71), 0),
        "cutoffs": draw_cutoffs(jax.random.fold_in(keys[6], 71), 0),
    }


OMEGA = 30.0


def row_cos(index, total):
    dist = jnp.maximum(jnp.minimum(index, total - 1 - index), 0)
    return jnp.sin(math.pi * (dist.astype(jnp.float32) + 0.5) / total)


def face_cos(face, total):
    dist = jnp.minimum(face, total - face)
    return jnp.sin(math.pi * dist.astype(jnp.float32) / total)


def spin_rate(index, total):
    return -2.0 * OMEGA * jnp.cos(math.pi * (index.astype(jnp.float32) + 0.5) / total)


def tendencies(xpad, ypad, cos_ext, cos_faces, coriolis, dlon, dlat):
    ux, vx, px, hx = xpad[0], xpad[1], xpad[2], xpad[3]
    uy, vy, py, hy = ypad[0], ypad[1], ypad[2], ypad[3]
    cos_mid = cos_ext[1:-1][:, None]
    heat_xp = px * hx
    heat_yp = py * hy
    east = 0.5 * (ux[..., :-1] + ux[..., 1:])
    mass_x = jnp.maximum(east, 0.0) * px[..., :-1] + jnp.minimum(east, 0.0) * px[..., 1:]
    heat_x = jnp.maximum(east, 0.0) * heat_xp[..., :-1] + jnp.minimum(east, 0.0) * heat_xp[..., 1:]
    north = 0.5 * (vy[..., :-1, :] + vy[..., 1:, :])
    faces = cos_faces[:, None]
    mass_y = faces * (jnp.maximum(north, 0.0) * py[..., :-1, :] + jnp.minimum(north, 0.0) * py[..., 1:, :])
    heat_y = faces * (jnp.maximum(north, 0.0) * heat_yp[..., :-1, :] + jnp.minimum(north, 0.0) * heat_yp[..., 1:, :])
    mass_t = -((mass_x[..., 1:] - mass_x[..., :-1]) / dlon + (mass_y[..., 1:, :] - mass_y[..., :-1, :]) / dlat) / cos_mid
    heat_t = -((heat_x[..., 1:] - heat_x[..., :-1]) / dlon + (heat_y[..., 1:, :] - heat_y[..., :-1, :]) / dlat) / cos_mid
    energy_x = 0.5 * (ux * ux + vx * vx) + heat_xp
    energy_y = 0.5 * (uy * uy + vy * vy) + heat_yp
    weighted = uy * cos_ext[:, None]
    spin = ((vx[..., 2:] - vx[..., :-2]) / (2.0 * dlon) - (weighted[..., 2:, :] - weighted[..., :-2, :]) / (2.0 * dlat)) / cos_mid
    absolute = coriolis[:, None] + spin
    u_mid = ux[..., 1:-1]
    v_mid = vx[..., 1:-1]
    u_t = absolute * v_mid - (energy_x[..., 2:] - energy_x[..., :-2]) / (2.0 * dlon * cos_mid)
    v_t = -absolute * u_mid - (energy_y[..., 2:, :] - energy_y[..., :-2, :]) / (2.0 * dlat)
    return jnp.stack([u_t, v_t, mass_t, heat_t])


def reference(u_wind, v_wind, thickness, theta, polar_rows, cutoffs):
    dlon = 2.0 * math.pi / NLON
    dlat = math.pi / NLAT
    step_size = 0.25 * dlon
    cos_ext = row_cos(jnp.arange(NLAT + 2) - 1, NLAT)
    cos_faces = face_cos(jnp.arange(NLAT + 1), NLAT)
    coriolis = spin_rate(jnp.arange(NLAT), NLAT)
    listed = jnp.any(polar_rows.reshape(-1)[None, :] == jnp.arange(NLAT)[:, None], axis=1)
    wave = jnp.arange(NLON // 2 + 1)
    keep = wave[None, :] <= cutoffs[:, None]
    signs = jnp.array([-1.0, -1.0, 1.0, 1.0], jnp.float32)[:, None]

    def one_level(level):
        fields = jnp.stack(level)
        south = jnp.roll(fields[:, 0, :], NLON // 2, axis=-1) * signs
        north = jnp.roll(fields[:, NLAT - 1, :], NLON // 2, axis=-1) * signs
        lat_padded = jnp.concatenate([south[:, None, :], fields, north[:, None, :]], axis=1)
        lon_padded = jnp.concatenate([fields[..., NLON - 1:], fields, fields[..., :1]], axis=-1)
        tend = tendencies(lon_padded, lat_padded, cos_ext, cos_faces, coriolis, dlon, dlat)
        spectrum = jnp.fft.rfft(tend, axis=-1)
        spectrum = jnp.where(keep[None, :, :], spectrum, jnp.zeros_like(spectrum))
        filtered = jnp.fft.irfft(spectrum, n=NLON, axis=-1).astype(tend.dtype)
        tend = jnp.where(listed[None, :, None], filtered, tend)
        return (level[0] + step_size * tend[0], level[1] + step_size * tend[1], level[2] + step_size * tend[2], level[2] * level[3] + step_size * tend[3])

    u_next, v_next, thickness_next, heat_next = lax.map(one_level, (u_wind, v_wind, thickness, theta))
    return (u_next, v_next, thickness_next, heat_next)
```

```python
import functools
import math

import jax
import jax.numpy as jnp
import numpy as np
from jax import lax
from jax.experimental import pallas as pl
from jax.experimental.pallas import tpu as pltpu
from jax.sharding import PartitionSpec as P

OMEGA = 30.0
KHALF = 208


def geometry(total_rows):
    row = np.arange(-1, total_rows + 1)
    dist = np.maximum(np.minimum(row, total_rows - 1 - row), 0)
    cos_row = np.sin(np.pi * (dist + 0.5) / total_rows)
    face = np.arange(total_rows + 1)
    cos_face = np.sin(np.pi * np.minimum(face, total_rows - face) / total_rows)
    spin = -2.0 * OMEGA * np.cos(np.pi * (np.arange(total_rows) + 0.5) / total_rows)
    table = np.zeros((total_rows, 8))
    table[:, 0] = cos_row[1:-1]
    table[:, 1] = cos_row[:-2]
    table[:, 2] = cos_row[2:]
    table[:, 3] = cos_face[:-1]
    table[:, 4] = cos_face[1:]
    table[:, 5] = spin
    table[:, 6] = 1.0 / cos_row[1:-1]
    return table.astype(np.float32)


def fourier_tables(total):
    column = np.arange(total // 2)
    tables = []
    for odd in (0, 1):
        wave = 2 * np.arange(KHALF) + odd
        angle = (column[:, None] * wave[None, :] % total) * (2.0 * np.pi / total)
        tables.append(np.concatenate([np.cos(angle), np.sin(angle)], axis=1))
    return [table.astype(np.float32) for table in tables]


def shifted(x, amount, axis, edge):
    size = x.shape[axis]
    place = lax.broadcasted_iota(jnp.int32, x.shape, axis)
    at = size - 1 if amount < 0 else 0
    return jnp.where(place == at, edge, pltpu.roll(x, amount % size, axis))


def tend_body(part, dlon, dlat, geo_ref, u_ref, v_ref, p_ref, h_ref, s_ref, n_ref, w_ref, e_ref, out_ref):
    geo = geo_ref[...]
    c0, cs, cn = geo[:, 0:1], geo[:, 1:2], geo[:, 2:3]
    fs, fn, spin0, inv = geo[:, 3:4], geo[:, 4:5], geo[:, 5:6], geo[:, 6:7]
    for k in range(u_ref.shape[0]):
        u, v, p, h = u_ref[k], v_ref[k], p_ref[k], h_ref[k]
        south = [s_ref[k, f : f + 1, :] for f in range(4)]
        north = [n_ref[k, f : f + 1, :] for f in range(4)]
        west = [w_ref[k, :, f : f + 1] for f in range(4)]
        east = [e_ref[k, :, f : f + 1] for f in range(4)]
        heat = p * h
        if part == 0:
            energy = 0.5 * (u * u + v * v) + heat
            edge = [0.5 * (q[0] * q[0] + q[1] * q[1]) + q[2] * q[3] for q in (south, north, west, east)]
            zeta = (shifted(v, -1, 1, east[1]) - shifted(v, 1, 1, west[1])) * (0.5 / dlon)
            zeta -= (cn * shifted(u, -1, 0, north[0]) - cs * shifted(u, 1, 0, south[0])) * (0.5 / dlat)
            absolute = spin0 + zeta * inv
            de_x = shifted(energy, -1, 1, edge[3]) - shifted(energy, 1, 1, edge[2])
            de_y = shifted(energy, -1, 0, edge[1]) - shifted(energy, 1, 0, edge[0])
            out_ref[0, 0, k] = absolute * v - de_x * ((0.5 / dlon) * inv)
            out_ref[0, 1, k] = -absolute * u - de_y * (0.5 / dlat)
        else:
            a = 0.5 * (u + shifted(u, -1, 1, east[0]))
            ap, am = jnp.maximum(a, 0.0), jnp.minimum(a, 0.0)
            mx = ap * p + am * shifted(p, -1, 1, east[2])
            hx = ap * heat + am * shifted(heat, -1, 1, east[2] * east[3])
            a0 = 0.5 * (west[0] + u[:, 0:1])
            ap0, am0 = jnp.maximum(a0, 0.0), jnp.minimum(a0, 0.0)
            mx0 = ap0 * west[2] + am0 * p[:, 0:1]
            hx0 = ap0 * (west[2] * west[3]) + am0 * heat[:, 0:1]
            b = 0.5 * (v + shifted(v, -1, 0, north[1]))
            bp, bm = fn * jnp.maximum(b, 0.0), fn * jnp.minimum(b, 0.0)
            my = bp * p + bm * shifted(p, -1, 0, north[2])
            hy = bp * heat + bm * shifted(heat, -1, 0, north[2] * north[3])
            b0 = 0.5 * (south[1] + v[0:1, :])
            bp0, bm0 = fs[0:1] * jnp.maximum(b0, 0.0), fs[0:1] * jnp.minimum(b0, 0.0)
            my0 = bp0 * south[2] + bm0 * p[0:1, :]
            hy0 = bp0 * (south[2] * south[3]) + bm0 * heat[0:1, :]
            out_ref[0, 0, k] = -inv * (
                (mx - shifted(mx, 1, 1, mx0)) * (1.0 / dlon) + (my - shifted(my, 1, 0, my0)) * (1.0 / dlat)
            )
            out_ref[0, 1, k] = -inv * (
                (hx - shifted(hx, 1, 1, hx0)) * (1.0 / dlon) + (hy - shifted(hy, 1, 0, hy0)) * (1.0 / dlat)
            )


def tendencies(part, groups, dlon, dlat, geo, fields, south, north, west, east):
    levels, rows, cols = fields[0].shape
    per = levels // groups
    field = pl.BlockSpec((per, rows, cols), lambda g: (g, 0, 0))
    lat_halo = pl.BlockSpec((per, 4, cols), lambda g: (g, 0, 0))
    lon_halo = pl.BlockSpec((per, rows, 4), lambda g: (g, 0, 0))
    return pl.pallas_call(
        functools.partial(tend_body, part, dlon, dlat),
        grid=(groups,),
        in_specs=[pl.BlockSpec((rows, 8), lambda g: (0, 0))] + [field] * 4 + [lat_halo] * 2 + [lon_halo] * 2,
        out_specs=pl.BlockSpec((1, 2, per, rows, cols), lambda g: (g, 0, 0, 0, 0)),
        out_shape=jax.ShapeDtypeStruct((groups, 2, per, rows, cols), jnp.float32),
        cost_estimate=pl.CostEstimate(flops=40 * levels * rows * cols, bytes_accessed=24 * levels * rows * cols, transcendentals=0),
    )(geo, *fields, south, north, west, east)


def per_device(u_wind, v_wind, thickness, theta, polar_rows, cutoffs):
    levels, rows, cols = u_wind.shape
    lat_count = lax.axis_size("lat")
    lon_count = lax.axis_size("lon")
    lat_place = lax.axis_index("lat")
    total_rows = rows * lat_count
    total_cols = cols * lon_count
    dlon = 2.0 * math.pi / total_cols
    dlat = math.pi / total_rows
    step_size = 0.25 * dlon
    high = lax.Precision.HIGH
    first_row = lat_place * rows
    fields = (u_wind, v_wind, thickness, theta)

    low_rows = jnp.stack([f[:, 0, :] for f in fields], axis=1)
    high_rows = jnp.stack([f[:, rows - 1, :] for f in fields], axis=1)
    south = lax.ppermute(high_rows, "lat", [(i, i + 1) for i in range(lat_count - 1)])
    north = lax.ppermute(low_rows, "lat", [(i + 1, i) for i in range(lat_count - 1)])
    polar = jnp.where(lat_place == 0, low_rows, high_rows)
    half = lon_count // 2
    pairs = [
        (band * lon_count + i, band * lon_count + (i + half) % lon_count)
        for band in (0, lat_count - 1)
        for i in range(lon_count)
    ]
    signs = jnp.array([-1.0, -1.0, 1.0, 1.0], jnp.float32)[None, :, None]
    polar = lax.ppermute(polar, ("lat", "lon"), pairs) * signs
    south = jnp.where(lat_place == 0, polar, south)
    north = jnp.where(lat_place == lat_count - 1, polar, north)
    ring = [(i, (i + 1) % lon_count) for i in range(lon_count)]
    west = lax.ppermute(jnp.stack([f[:, :, cols - 1] for f in fields]), "lon", ring)
    east = lax.ppermute(jnp.stack([f[:, :, 0] for f in fields]), "lon", [(j, i) for i, j in ring])
    west = jnp.transpose(west, (1, 2, 0))
    east = jnp.transpose(east, (1, 2, 0))
    geo = lax.dynamic_slice_in_dim(jnp.asarray(geometry(total_rows)), first_row, rows, 0)

    own = first_row + jnp.arange(rows)
    listed = jnp.any(polar_rows.reshape(-1)[None, :] == own[:, None], axis=1)[:, None]
    limit = lax.dynamic_slice_in_dim(cutoffs, first_row, rows, 0)
    tables = [jnp.asarray(t).reshape(lon_count // 2, cols, 2 * KHALF) for t in fourier_tables(total_cols)]
    weights = []
    for odd in (0, 1):
        wave = 2 * jnp.arange(KHALF) + odd
        w = jnp.where(wave[None, :] == 0, 1.0, jnp.where(wave[None, :] <= limit[:, None], 2.0, 0.0)) / total_cols
        weights.append(jnp.concatenate([w, w], axis=1))

    def filtered(tend):
        per = levels // lon_count
        got = lax.all_to_all(tend, "lon", 0, 0, tiled=True)
        front, back = got[:half], got[half:]
        sides = []
        for x, table, weight in ((front + back, tables[0], weights[0]), (front - back, tables[1], weights[1])):
            spectrum = jnp.einsum("bflrc,bck->flrk", x, table, precision=high, preferred_element_type=jnp.float32)
            spectrum = spectrum * weight
            sides.append(
                jnp.einsum("flrk,bck->bflrc", spectrum, table, precision=high, preferred_element_type=jnp.float32)
            )
        out = jnp.concatenate([sides[0] + sides[1], sides[0] - sides[1]], axis=0)
        return lax.all_to_all(out, "lon", 0, 0, tiled=True)

    final = []
    for part in (0, 1):
        tend = tendencies(part, lon_count, dlon, dlat, geo, fields, south, north, west, east)
        chosen = jnp.where(listed, filtered(tend), tend)
        final += [chosen[:, q].reshape(levels, rows, cols) for q in (0, 1)]
    return (
        u_wind + step_size * final[0],
        v_wind + step_size * final[1],
        thickness + step_size * final[2],
        thickness * theta + step_size * final[3],
    )


def solution(mesh):
    field = P(None, "lat", "lon")
    return jax.shard_map(
        per_device,
        mesh=mesh,
        in_specs=(field, field, field, field, P(), P()),
        out_specs=(field, field, field, field),
        check_vma=False,
    )
```

```python
import functools
import math

import jax
import jax.numpy as jnp
import numpy as np
from jax import lax
from jax.experimental import pallas as pl
from jax.experimental.pallas import tpu as pltpu
from jax.sharding import PartitionSpec as P

OMEGA = 30.0
KHALF = 208
LANES = 128


def geometry(total_rows):
    row = np.arange(-1, total_rows + 1)
    dist = np.maximum(np.minimum(row, total_rows - 1 - row), 0)
    cos_row = np.sin(np.pi * (dist + 0.5) / total_rows)
    face = np.arange(total_rows + 1)
    cos_face = np.sin(np.pi * np.minimum(face, total_rows - face) / total_rows)
    spin = -2.0 * OMEGA * np.cos(np.pi * (np.arange(total_rows) + 0.5) / total_rows)
    table = np.zeros((total_rows, 8))
    table[:, 0] = cos_row[1:-1]
    table[:, 1] = cos_row[:-2]
    table[:, 2] = cos_row[2:]
    table[:, 3] = cos_face[:-1]
    table[:, 4] = cos_face[1:]
    table[:, 5] = spin
    table[:, 6] = 1.0 / cos_row[1:-1]
    return table.astype(np.float32)


def fourier_tables(total):
    column = np.arange(total // 2)
    tables = []
    for odd in (0, 1):
        wave = 2 * np.arange(KHALF) + odd
        angle = (column[:, None] * wave[None, :] % total) * (2.0 * np.pi / total)
        tables.append(np.concatenate([np.cos(angle), np.sin(angle)], axis=1))
    return [table.astype(np.float32) for table in tables]


def copy_all(pairs, sems):
    copies = [pltpu.make_async_copy(src, dst, sems.at[i]) for i, (src, dst) in enumerate(pairs)]
    for copy in copies:
        copy.start()
    for copy in copies:
        copy.wait()


def pack_body(count, chunk, halo_chunks, rows, me_ref, *refs):
    fields = refs[:4]
    halo = refs[4] if halo_chunks else None
    outs, sems = refs[-count - 1 : -1], refs[-1]
    me = me_ref[0]
    pairs = []
    for step in range(count):
        level = lax.rem(me + step, count)
        for f in range(4):
            pairs.append((fields[f].at[chunk * count + level], outs[step].at[pl.ds(f * rows, rows)]))
        for k, c in enumerate(halo_chunks):
            pairs.append((halo.at[c * count + level], outs[step].at[pl.ds(4 * rows + 8 * k, 8)]))
    copy_all(pairs, sems)


def pack(count, chunk, halo_chunks, me, fields, halo):
    _, rows, cols = fields[0].shape
    height = 4 * rows + 8 * len(halo_chunks)
    anywhere = pl.BlockSpec(memory_space=pl.ANY)
    operands = list(fields) + ([halo] if halo_chunks else [])
    return pl.pallas_call(
        functools.partial(pack_body, count, chunk, halo_chunks, rows),
        in_specs=[pl.BlockSpec(memory_space=pltpu.SMEM)] + [anywhere] * len(operands),
        out_specs=[anywhere] * count,
        out_shape=[jax.ShapeDtypeStruct((height, cols), jnp.float32)] * count,
        scratch_shapes=[pltpu.SemaphoreType.DMA((count * (4 + len(halo_chunks)),))],
        cost_estimate=pl.CostEstimate(flops=0, bytes_accessed=8 * count * height * cols, transcendentals=0),
    )(me, *operands)


def place_body(count, chunk, rows, me_ref, *refs):
    blocks, outs, sems = refs[:count], refs[-5:-1], refs[-1]
    me = me_ref[0]
    pairs = []
    for step in range(count):
        level = chunk * count + lax.rem(me + count - step, count)
        for f in range(4):
            pairs.append((blocks[step].at[pl.ds(f * rows, rows)], outs[f].at[level]))
    copy_all(pairs, sems)


def place(chunk, me, blocks, earlier, shape):
    count = len(blocks)
    anywhere = pl.BlockSpec(memory_space=pl.ANY)
    operands = list(blocks) + list(earlier)
    return pl.pallas_call(
        functools.partial(place_body, count, chunk, shape[1]),
        in_specs=[pl.BlockSpec(memory_space=pltpu.SMEM)] + [anywhere] * len(operands),
        out_specs=[anywhere] * 4,
        out_shape=[jax.ShapeDtypeStruct(shape, jnp.float32)] * 4,
        scratch_shapes=[pltpu.SemaphoreType.DMA((4 * count,))],
        input_output_aliases={1 + count + f: f for f in range(4)} if earlier else {},
        cost_estimate=pl.CostEstimate(flops=0, bytes_accessed=32 * count * shape[1] * shape[2], transcendentals=0),
    )(me, *operands)


def lat_shift(x, amount, edge):
    size = x.shape[0]
    place = lax.broadcasted_iota(jnp.int32, x.shape, 0)
    at = size - 1 if amount < 0 else 0
    return jnp.where(place == at, edge, pltpu.roll(x, amount % size, 0))


def tend_body(count, rows, cols, dlon, dlat, where_ref, geo_ref, *refs):
    blocks, halos = refs[:count], refs[count : 2 * count]
    tend_ref, even_ref, odd_ref = refs[2 * count :]
    is_first, is_last = where_ref[0] == 1, where_ref[1] == 1
    geo = geo_ref[...]
    cs, cn = geo[:, 1:2], geo[:, 2:3]
    fs, fn, spin0, inv = geo[0:1, 3:4], geo[:, 4:5], geo[:, 5:6], geo[:, 6:7]
    wide = cols + 2 * LANES
    signs = (-1.0, -1.0, 1.0, 1.0)

    def mid(x):
        return x[:, LANES : LANES + cols]

    def east_of(x):
        return pltpu.roll(x, wide - 1, 1)

    def west_of(x):
        return pltpu.roll(x, 1, 1)

    for r in range(count):
        prev, here, nxt = blocks[r - 1], blocks[r], blocks[(r + 1) % count]
        across = blocks[(r + count // 2) % count]
        ext = []
        south, north = [], []
        for f in range(4):
            part = slice(f * rows, (f + 1) * rows)
            ext.append(jnp.concatenate([prev[part, cols - LANES :], here[part, :], nxt[part, :LANES]], axis=1))
            low, high = f * rows, (f + 1) * rows - 1
            south.append(jnp.where(is_first, signs[f] * across[low : low + 1, :], halos[r][f : f + 1, :]))
            north.append(jnp.where(is_last, signs[f] * across[high : high + 1, :], halos[r][4 + f : 5 + f, :]))
        ux, vx, px, hx = ext
        heat_x = px * hx
        energy_x = 0.5 * (ux * ux + vx * vx) + heat_x
        u, v, p, heat, energy = mid(ux), mid(vx), mid(px), mid(heat_x), mid(energy_x)
        out = slice(r * cols, (r + 1) * cols)

        zeta = (mid(east_of(vx)) - mid(west_of(vx))) * (0.5 / dlon)
        zeta -= (cn * lat_shift(u, -1, north[0]) - cs * lat_shift(u, 1, south[0])) * (0.5 / dlat)
        absolute = spin0 + zeta * inv
        edges = [0.5 * (q[0] * q[0] + q[1] * q[1]) + q[2] * q[3] for q in (south, north)]
        de_x = mid(east_of(energy_x)) - mid(west_of(energy_x))
        de_y = lat_shift(energy, -1, edges[1]) - lat_shift(energy, 1, edges[0])
        tend_ref[0:rows, out] = absolute * v - de_x * ((0.5 / dlon) * inv)
        tend_ref[rows : 2 * rows, out] = -absolute * u - de_y * (0.5 / dlat)

        a = 0.5 * (ux + east_of(ux))
        ap, am = jnp.maximum(a, 0.0), jnp.minimum(a, 0.0)
        flow_x = ap * px + am * east_of(px)
        hot_x = ap * heat_x + am * east_of(heat_x)
        b = 0.5 * (v + lat_shift(v, -1, north[1]))
        bp, bm = fn * jnp.maximum(b, 0.0), fn * jnp.minimum(b, 0.0)
        flow_y = bp * p + bm * lat_shift(p, -1, north[2])
        hot_y = bp * heat + bm * lat_shift(heat, -1, north[2] * north[3])
        b0 = 0.5 * (south[1] + v[0:1, :])
        bp0, bm0 = fs * jnp.maximum(b0, 0.0), fs * jnp.minimum(b0, 0.0)
        flow_y0 = bp0 * south[2] + bm0 * p[0:1, :]
        hot_y0 = bp0 * (south[2] * south[3]) + bm0 * heat[0:1, :]
        tend_ref[2 * rows : 3 * rows, out] = -inv * (
            (mid(flow_x) - mid(west_of(flow_x))) * (1.0 / dlon) + (flow_y - lat_shift(flow_y, 1, flow_y0)) * (1.0 / dlat)
        )
        tend_ref[3 * rows : 4 * rows, out] = -inv * (
            (mid(hot_x) - mid(west_of(hot_x))) * (1.0 / dlon) + (hot_y - lat_shift(hot_y, 1, hot_y0)) * (1.0 / dlat)
        )
    half = count * cols // 2
    for r in range(count // 2):
        near = tend_ref[:, r * cols : (r + 1) * cols]
        far = tend_ref[:, half + r * cols : half + (r + 1) * cols]
        even_ref[:, r * cols : (r + 1) * cols] = near + far
        odd_ref[:, r * cols : (r + 1) * cols] = near - far


def tendencies(rows, dlon, dlat, ends, geo, blocks, halo_blocks, halo_slot):
    count = len(blocks)
    cols = blocks[0].shape[1]
    full = count * cols
    high = 4 * rows
    return pl.pallas_call(
        functools.partial(tend_body, count, rows, cols, dlon, dlat),
        grid=(1,),
        in_specs=[pl.BlockSpec(memory_space=pltpu.SMEM), pl.BlockSpec((rows, 8), lambda g: (0, 0))]
        + [pl.BlockSpec((high, cols), lambda g: (0, 0))] * count
        + [pl.BlockSpec((8, cols), lambda g: (high // 8 + halo_slot, 0))] * count,
        out_specs=[
            pl.BlockSpec((high, full), lambda g: (0, 0)),
            pl.BlockSpec((high, full // 2), lambda g: (0, 0)),
            pl.BlockSpec((high, full // 2), lambda g: (0, 0)),
        ],
        out_shape=[
            jax.ShapeDtypeStruct((high, full), jnp.float32),
            jax.ShapeDtypeStruct((high, full // 2), jnp.float32),
            jax.ShapeDtypeStruct((high, full // 2), jnp.float32),
        ],
        compiler_params=pltpu.CompilerParams(vmem_limit_bytes=32 * 1024 * 1024),
        cost_estimate=pl.CostEstimate(flops=40 * high * full, bytes_accessed=12 * high * full, transcendentals=0),
    )(ends, geo, *blocks, *halo_blocks)


def update_body(count, rows, cols, step_size, listed_ref, tend_ref, even_ref, odd_ref, *refs):
    blocks, outs = refs[:count], refs[count:]
    listed = listed_ref[...] > 0
    half = count // 2
    for r in range(count):
        src = slice((r % half) * cols, (r % half + 1) * cols)
        for f in range(4):
            part = slice(f * rows, (f + 1) * rows)
            if r < half:
                smooth = even_ref[part, src] + odd_ref[part, src]
            else:
                smooth = even_ref[part, src] - odd_ref[part, src]
            chosen = jnp.where(listed, smooth, tend_ref[part, r * cols : (r + 1) * cols])
            base = blocks[r][part, :]
            if f == 3:
                base = base * blocks[r][2 * rows : 3 * rows, :]
            outs[r][part, :] = base + step_size * chosen


def updated(rows, step_size, listed, tend, even, odd, blocks):
    count = len(blocks)
    cols = blocks[0].shape[1]
    high = 4 * rows
    whole = lambda shape: pl.BlockSpec(shape, lambda g: (0, 0))
    return pl.pallas_call(
        functools.partial(update_body, count, rows, cols, step_size),
        grid=(1,),
        in_specs=[whole((rows, 1)), whole(tend.shape), whole(even.shape), whole(odd.shape)] + [whole((high, cols))] * count,
        out_specs=[whole((high, cols))] * count,
        out_shape=[jax.ShapeDtypeStruct((high, cols), jnp.float32)] * count,
        compiler_params=pltpu.CompilerParams(vmem_limit_bytes=32 * 1024 * 1024),
        cost_estimate=pl.CostEstimate(flops=4 * high * count * cols, bytes_accessed=16 * high * count * cols, transcendentals=0),
    )(listed, tend, even, odd, *blocks)


def per_device(u_wind, v_wind, thickness, theta, polar_rows, cutoffs):
    levels, rows, cols = u_wind.shape
    lat_count = lax.axis_size("lat")
    count = lax.axis_size("lon")
    lat_place = lax.axis_index("lat")
    total_rows = rows * lat_count
    total_cols = cols * count
    dlon = 2.0 * math.pi / total_cols
    dlat = math.pi / total_rows
    step_size = 0.25 * dlon
    first_row = lat_place * rows
    fields = (u_wind, v_wind, thickness, theta)
    me = lax.axis_index("lon").astype(jnp.int32).reshape(1)
    chunks = levels // count

    def exchanged(blocks):
        return [blocks[0]] + [
            lax.ppermute(blocks[step], "lon", [(i, (i + step) % count) for i in range(count)])
            for step in range(1, count)
        ]

    def circle(received):
        return [received[(count - r) % count] for r in range(count)]

    first = circle(exchanged(pack(count, 0, (), me, fields, None)))
    low_rows = jnp.stack([f[:, 0, :] for f in fields], axis=1)
    high_rows = jnp.stack([f[:, rows - 1, :] for f in fields], axis=1)
    south = lax.ppermute(high_rows, "lat", [(i, i + 1) for i in range(lat_count - 1)])
    north = lax.ppermute(low_rows, "lat", [(i + 1, i) for i in range(lat_count - 1)])
    halo = jnp.concatenate([south, north], axis=1)
    circles = [first]
    for c in range(1, chunks):
        carried = (0, 1) if c == 1 else (c,)
        circles.append(circle(exchanged(pack(count, c, carried, me, fields, halo))))
    halo_at = [(1, 0), (1, 1)] + [(c, 0) for c in range(2, chunks)]

    geo = lax.dynamic_slice_in_dim(jnp.asarray(geometry(total_rows)), first_row, rows, 0)
    own = first_row + jnp.arange(rows)
    listed = jnp.any(polar_rows.reshape(-1)[None, :] == own[:, None], axis=1)[:, None].astype(jnp.int32)
    limit = jnp.tile(lax.dynamic_slice_in_dim(cutoffs, first_row, rows, 0), 4)
    ends = jnp.stack([lat_place == 0, lat_place == lat_count - 1]).astype(jnp.int32)
    tables = [jnp.asarray(t) for t in fourier_tables(total_cols)]
    weights = []
    for odd in (0, 1):
        wave = 2 * jnp.arange(KHALF) + odd
        w = jnp.where(wave[None, :] == 0, 1.0, jnp.where(wave[None, :] <= limit[:, None], 2.0, 0.0)) / total_cols
        weights.append(jnp.concatenate([w, w], axis=1))

    done = ()
    high = lax.Precision.HIGH
    for c in range(chunks):
        source, slot = halo_at[c]
        tend, *sides = tendencies(rows, dlon, dlat, ends, geo, circles[c], circles[source], slot)
        smooth = []
        for x, table, weight in zip(sides, tables, weights):
            spectrum = jnp.dot(x, table, precision=high, preferred_element_type=jnp.float32) * weight
            smooth.append(jnp.dot(spectrum, table.T, precision=high, preferred_element_type=jnp.float32))
        fresh = updated(rows, step_size, listed, tend, *smooth, circles[c])
        done = place(c, me, exchanged(fresh), done, (levels, rows, cols))
    return tuple(done)


def solution(mesh):
    field = P(None, "lat", "lon")
    return jax.shard_map(
        per_device,
        mesh=mesh,
        in_specs=(field, field, field, field, P(), P()),
        out_specs=(field, field, field, field),
        check_vma=False,
    )
```

```python
import functools
import math

import jax
import jax.numpy as jnp
import numpy as np
from jax import lax
from jax.experimental import pallas as pl
from jax.experimental.pallas import tpu as pltpu
from jax.sharding import PartitionSpec as P

OMEGA = 30.0
KHALF = 208
LANES = 128


def geometry(total_rows):
    row = np.arange(-1, total_rows + 1)
    dist = np.maximum(np.minimum(row, total_rows - 1 - row), 0)
    cos_row = np.sin(np.pi * (dist + 0.5) / total_rows)
    face = np.arange(total_rows + 1)
    cos_face = np.sin(np.pi * np.minimum(face, total_rows - face) / total_rows)
    spin = -2.0 * OMEGA * np.cos(np.pi * (np.arange(total_rows) + 0.5) / total_rows)
    table = np.zeros((total_rows, 8))
    table[:, 0] = cos_row[1:-1]
    table[:, 1] = cos_row[:-2]
    table[:, 2] = cos_row[2:]
    table[:, 3] = cos_face[:-1]
    table[:, 4] = cos_face[1:]
    table[:, 5] = spin
    table[:, 6] = 1.0 / cos_row[1:-1]
    return table.astype(np.float32)


def fourier_tables(total):
    column = np.arange(total // 2)
    tables = []
    for odd in (0, 1):
        wave = 2 * np.arange(KHALF) + odd
        angle = (column[:, None] * wave[None, :] % total) * (2.0 * np.pi / total)
        tables.append(np.concatenate([np.cos(angle), np.sin(angle)], axis=1))
    return [table.astype(np.float32) for table in tables]


def pack_body(count, halo_chunks, rows, me_ref, *refs):
    fields, halos, outs = refs[:4], refs[4 : 4 + len(halo_chunks)], refs[4 + len(halo_chunks) :]
    me = me_ref[0]
    for step in range(count):
        level = lax.rem(me + step, count)
        for f in range(4):
            outs[step][f * rows : (f + 1) * rows, :] = fields[f][level]
        for k in range(len(halo_chunks)):
            outs[step][4 * rows + 8 * k : 4 * rows + 8 * k + 8, :] = halos[k][level]


def pack(count, chunk, halo_chunks, me, fields, halo):
    _, rows, cols = fields[0].shape
    height = 4 * rows + 8 * len(halo_chunks)
    whole = pl.BlockSpec((height, cols), lambda g: (0, 0))
    return pl.pallas_call(
        functools.partial(pack_body, count, halo_chunks, rows),
        grid=(1,),
        in_specs=[pl.BlockSpec(memory_space=pltpu.SMEM)]
        + [pl.BlockSpec((count, rows, cols), lambda g: (chunk, 0, 0))] * 4
        + [pl.BlockSpec((count, 8, cols), functools.partial(lambda c, g: (c, 0, 0), c)) for c in halo_chunks],
        out_specs=[whole] * count,
        out_shape=[jax.ShapeDtypeStruct((height, cols), jnp.float32)] * count,
        compiler_params=pltpu.CompilerParams(vmem_limit_bytes=32 * 1024 * 1024),
        cost_estimate=pl.CostEstimate(flops=0, bytes_accessed=8 * count * height * cols, transcendentals=0),
    )(me, *fields, *([halo] * len(halo_chunks)))


def place_body(count, rows, me_ref, *refs):
    blocks, outs = refs[:count], refs[-4:]
    me = me_ref[0]
    for step in range(count):
        level = lax.rem(me + count - step, count)
        for f in range(4):
            outs[f][level] = blocks[step][f * rows : (f + 1) * rows, :]


def place(chunk, me, blocks, earlier, shape):
    count = len(blocks)
    _, rows, cols = shape
    return pl.pallas_call(
        functools.partial(place_body, count, rows),
        grid=(1,),
        in_specs=[pl.BlockSpec(memory_space=pltpu.SMEM)]
        + [pl.BlockSpec((4 * rows, cols), lambda g: (0, 0))] * count
        + [pl.BlockSpec(memory_space=pl.ANY)] * len(earlier),
        out_specs=[pl.BlockSpec((count, rows, cols), lambda g: (chunk, 0, 0))] * 4,
        out_shape=[jax.ShapeDtypeStruct(shape, jnp.float32)] * 4,
        input_output_aliases={1 + count + f: f for f in range(4)} if earlier else {},
        compiler_params=pltpu.CompilerParams(vmem_limit_bytes=32 * 1024 * 1024),
        cost_estimate=pl.CostEstimate(flops=0, bytes_accessed=32 * count * rows * cols, transcendentals=0),
    )(me, *blocks, *earlier)


def lat_shift(x, amount, edge):
    size = x.shape[0]
    place = lax.broadcasted_iota(jnp.int32, x.shape, 0)
    at = size - 1 if amount < 0 else 0
    return jnp.where(place == at, edge, pltpu.roll(x, amount % size, 0))


def tend_body(count, rows, cols, dlon, dlat, where_ref, geo_ref, *refs):
    blocks, halos = refs[:count], refs[count : 2 * count]
    tend_ref, even_ref, odd_ref = refs[2 * count :]
    is_first, is_last = where_ref[0] == 1, where_ref[1] == 1
    geo = geo_ref[...]
    cs, cn = geo[:, 1:2], geo[:, 2:3]
    fs, fn, spin0, inv = geo[0:1, 3:4], geo[:, 4:5], geo[:, 5:6], geo[:, 6:7]
    wide = cols + 2 * LANES
    signs = (-1.0, -1.0, 1.0, 1.0)

    def mid(x):
        return x[:, LANES : LANES + cols]

    def east_of(x):
        return pltpu.roll(x, wide - 1, 1)

    def west_of(x):
        return pltpu.roll(x, 1, 1)

    for r in range(count):
        prev, here, nxt = blocks[r - 1], blocks[r], blocks[(r + 1) % count]
        across = blocks[(r + count // 2) % count]
        ext = []
        south, north = [], []
        for f in range(4):
            part = slice(f * rows, (f + 1) * rows)
            ext.append(jnp.concatenate([prev[part, cols - LANES :], here[part, :], nxt[part, :LANES]], axis=1))
            low, high = f * rows, (f + 1) * rows - 1
            south.append(jnp.where(is_first, signs[f] * across[low : low + 1, :], halos[r][f : f + 1, :]))
            north.append(jnp.where(is_last, signs[f] * across[high : high + 1, :], halos[r][4 + f : 5 + f, :]))
        ux, vx, px, hx = ext
        heat_x = px * hx
        energy_x = 0.5 * (ux * ux + vx * vx) + heat_x
        u, v, p, heat, energy = mid(ux), mid(vx), mid(px), mid(heat_x), mid(energy_x)
        out = slice(r * cols, (r + 1) * cols)

        zeta = (mid(east_of(vx)) - mid(west_of(vx))) * (0.5 / dlon)
        zeta -= (cn * lat_shift(u, -1, north[0]) - cs * lat_shift(u, 1, south[0])) * (0.5 / dlat)
        absolute = spin0 + zeta * inv
        edges = [0.5 * (q[0] * q[0] + q[1] * q[1]) + q[2] * q[3] for q in (south, north)]
        de_x = mid(east_of(energy_x)) - mid(west_of(energy_x))
        de_y = lat_shift(energy, -1, edges[1]) - lat_shift(energy, 1, edges[0])
        tend_ref[0:rows, out] = absolute * v - de_x * ((0.5 / dlon) * inv)
        tend_ref[rows : 2 * rows, out] = -absolute * u - de_y * (0.5 / dlat)

        a = 0.5 * (ux + east_of(ux))
        ap, am = jnp.maximum(a, 0.0), jnp.minimum(a, 0.0)
        flow_x = ap * px + am * east_of(px)
        hot_x = ap * heat_x + am * east_of(heat_x)
        b = 0.5 * (v + lat_shift(v, -1, north[1]))
        bp, bm = fn * jnp.maximum(b, 0.0), fn * jnp.minimum(b, 0.0)
        flow_y = bp * p + bm * lat_shift(p, -1, north[2])
        hot_y = bp * heat + bm * lat_shift(heat, -1, north[2] * north[3])
        b0 = 0.5 * (south[1] + v[0:1, :])
        bp0, bm0 = fs * jnp.maximum(b0, 0.0), fs * jnp.minimum(b0, 0.0)
        flow_y0 = bp0 * south[2] + bm0 * p[0:1, :]
        hot_y0 = bp0 * (south[2] * south[3]) + bm0 * heat[0:1, :]
        tend_ref[2 * rows : 3 * rows, out] = -inv * (
            (mid(flow_x) - mid(west_of(flow_x))) * (1.0 / dlon) + (flow_y - lat_shift(flow_y, 1, flow_y0)) * (1.0 / dlat)
        )
        tend_ref[3 * rows : 4 * rows, out] = -inv * (
            (mid(hot_x) - mid(west_of(hot_x))) * (1.0 / dlon) + (hot_y - lat_shift(hot_y, 1, hot_y0)) * (1.0 / dlat)
        )
    half = count * cols // 2
    for r in range(count // 2):
        near = tend_ref[:, r * cols : (r + 1) * cols]
        far = tend_ref[:, half + r * cols : half + (r + 1) * cols]
        even_ref[:, r * cols : (r + 1) * cols] = near + far
        odd_ref[:, r * cols : (r + 1) * cols] = near - far


def tendencies(rows, dlon, dlat, ends, geo, blocks, halo_blocks, halo_slot):
    count = len(blocks)
    cols = blocks[0].shape[1]
    full = count * cols
    high = 4 * rows
    return pl.pallas_call(
        functools.partial(tend_body, count, rows, cols, dlon, dlat),
        grid=(1,),
        in_specs=[pl.BlockSpec(memory_space=pltpu.SMEM), pl.BlockSpec((rows, 8), lambda g: (0, 0))]
        + [pl.BlockSpec((high, cols), lambda g: (0, 0))] * count
        + [pl.BlockSpec((8, cols), lambda g: (high // 8 + halo_slot, 0))] * count,
        out_specs=[
            pl.BlockSpec((high, full), lambda g: (0, 0)),
            pl.BlockSpec((high, full // 2), lambda g: (0, 0)),
            pl.BlockSpec((high, full // 2), lambda g: (0, 0)),
        ],
        out_shape=[
            jax.ShapeDtypeStruct((high, full), jnp.float32),
            jax.ShapeDtypeStruct((high, full // 2), jnp.float32),
            jax.ShapeDtypeStruct((high, full // 2), jnp.float32),
        ],
        compiler_params=pltpu.CompilerParams(vmem_limit_bytes=32 * 1024 * 1024),
        cost_estimate=pl.CostEstimate(flops=40 * high * full, bytes_accessed=12 * high * full, transcendentals=0),
    )(ends, geo, *blocks, *halo_blocks)


def update_body(count, rows, cols, step_size, listed_ref, tend_ref, even_ref, odd_ref, *refs):
    blocks, outs = refs[:count], refs[count:]
    listed = listed_ref[...] > 0
    half = count // 2
    for r in range(count):
        src = slice((r % half) * cols, (r % half + 1) * cols)
        for f in range(4):
            part = slice(f * rows, (f + 1) * rows)
            if r < half:
                smooth = even_ref[part, src] + odd_ref[part, src]
            else:
                smooth = even_ref[part, src] - odd_ref[part, src]
            chosen = jnp.where(listed, smooth, tend_ref[part, r * cols : (r + 1) * cols])
            base = blocks[r][part, :]
            if f == 3:
                base = base * blocks[r][2 * rows : 3 * rows, :]
            outs[r][part, :] = base + step_size * chosen


def updated(rows, step_size, listed, tend, even, odd, blocks):
    count = len(blocks)
    cols = blocks[0].shape[1]
    high = 4 * rows
    whole = lambda shape: pl.BlockSpec(shape, lambda g: (0, 0))
    return pl.pallas_call(
        functools.partial(update_body, count, rows, cols, step_size),
        grid=(1,),
        in_specs=[whole((rows, 1)), whole(tend.shape), whole(even.shape), whole(odd.shape)] + [whole((high, cols))] * count,
        out_specs=[whole((high, cols))] * count,
        out_shape=[jax.ShapeDtypeStruct((high, cols), jnp.float32)] * count,
        compiler_params=pltpu.CompilerParams(vmem_limit_bytes=32 * 1024 * 1024),
        cost_estimate=pl.CostEstimate(flops=4 * high * count * cols, bytes_accessed=16 * high * count * cols, transcendentals=0),
    )(listed, tend, even, odd, *blocks)


def per_device(u_wind, v_wind, thickness, theta, polar_rows, cutoffs):
    levels, rows, cols = u_wind.shape
    lat_count = lax.axis_size("lat")
    count = lax.axis_size("lon")
    lat_place = lax.axis_index("lat")
    total_rows = rows * lat_count
    total_cols = cols * count
    dlon = 2.0 * math.pi / total_cols
    dlat = math.pi / total_rows
    step_size = 0.25 * dlon
    first_row = lat_place * rows
    fields = (u_wind, v_wind, thickness, theta)
    me = lax.axis_index("lon").astype(jnp.int32).reshape(1)
    chunks = levels // count

    def exchanged(blocks):
        return [blocks[0]] + [
            lax.ppermute(blocks[step], "lon", [(i, (i + step) % count) for i in range(count)])
            for step in range(1, count)
        ]

    def circle(received):
        return [received[(count - r) % count] for r in range(count)]

    first = circle(exchanged(pack(count, 0, (), me, fields, None)))
    low_rows = jnp.stack([f[:, 0, :] for f in fields], axis=1)
    high_rows = jnp.stack([f[:, rows - 1, :] for f in fields], axis=1)
    south = lax.ppermute(high_rows, "lat", [(i, i + 1) for i in range(lat_count - 1)])
    north = lax.ppermute(low_rows, "lat", [(i + 1, i) for i in range(lat_count - 1)])
    halo = jnp.concatenate([south, north], axis=1)
    circles = [first]
    for c in range(1, chunks):
        carried = (0, 1) if c == 1 else (c,)
        circles.append(circle(exchanged(pack(count, c, carried, me, fields, halo))))
    halo_at = [(1, 0), (1, 1)] + [(c, 0) for c in range(2, chunks)]

    geo = lax.dynamic_slice_in_dim(jnp.asarray(geometry(total_rows)), first_row, rows, 0)
    own = first_row + jnp.arange(rows)
    listed = jnp.any(polar_rows.reshape(-1)[None, :] == own[:, None], axis=1)[:, None].astype(jnp.int32)
    limit = jnp.tile(lax.dynamic_slice_in_dim(cutoffs, first_row, rows, 0), 4)
    ends = jnp.stack([lat_place == 0, lat_place == lat_count - 1]).astype(jnp.int32)
    tables = [jnp.asarray(t) for t in fourier_tables(total_cols)]
    weights = []
    for odd in (0, 1):
        wave = 2 * jnp.arange(KHALF) + odd
        w = jnp.where(wave[None, :] == 0, 1.0, jnp.where(wave[None, :] <= limit[:, None], 2.0, 0.0)) / total_cols
        weights.append(jnp.concatenate([w, w], axis=1))

    done = ()
    high = lax.Precision.HIGH
    for c in range(chunks):
        source, slot = halo_at[c]
        tend, *sides = tendencies(rows, dlon, dlat, ends, geo, circles[c], circles[source], slot)
        smooth = []
        for x, table, weight in zip(sides, tables, weights):
            spectrum = jnp.dot(x, table, precision=high, preferred_element_type=jnp.float32) * weight
            smooth.append(jnp.dot(spectrum, table.T, precision=high, preferred_element_type=jnp.float32))
        fresh = updated(rows, step_size, listed, tend, *smooth, circles[c])
        done = place(c, me, exchanged(fresh), done, (levels, rows, cols))
    return tuple(done)


def solution(mesh):
    field = P(None, "lat", "lon")
    return jax.shard_map(
        per_device,
        mesh=mesh,
        in_specs=(field, field, field, field, P(), P()),
        out_specs=(field, field, field, field),
        check_vma=False,
    )
```

```python
import functools
import math

import jax
import jax.numpy as jnp
import numpy as np
from jax import lax
from jax.experimental import pallas as pl
from jax.experimental.pallas import tpu as pltpu
from jax.sharding import PartitionSpec as P

OMEGA = 30.0
KHALF = 208
LANES = 128


def geometry(total_rows):
    row = np.arange(-1, total_rows + 1)
    dist = np.maximum(np.minimum(row, total_rows - 1 - row), 0)
    cos_row = np.sin(np.pi * (dist + 0.5) / total_rows)
    face = np.arange(total_rows + 1)
    cos_face = np.sin(np.pi * np.minimum(face, total_rows - face) / total_rows)
    spin = -2.0 * OMEGA * np.cos(np.pi * (np.arange(total_rows) + 0.5) / total_rows)
    table = np.zeros((total_rows, 8))
    table[:, 0] = cos_row[1:-1]
    table[:, 1] = cos_row[:-2]
    table[:, 2] = cos_row[2:]
    table[:, 3] = cos_face[:-1]
    table[:, 4] = cos_face[1:]
    table[:, 5] = spin
    table[:, 6] = 1.0 / cos_row[1:-1]
    return table.astype(np.float32)


def fourier_tables(total):
    column = np.arange(total // 2)
    tables = []
    for odd in (0, 1):
        wave = 2 * np.arange(KHALF) + odd
        angle = (column[:, None] * wave[None, :] % total) * (2.0 * np.pi / total)
        tables.append(np.concatenate([np.cos(angle), np.sin(angle)], axis=1))
    return [table.astype(np.float32) for table in tables]


def copy_all(pairs, sems):
    copies = [pltpu.make_async_copy(src, dst, sems.at[i]) for i, (src, dst) in enumerate(pairs)]
    for copy in copies:
        copy.start()
    for copy in copies:
        copy.wait()


def pack_body(first, per, rows, *refs):
    fields, out, sems = refs[:4], refs[4], refs[5]
    count = out.shape[0]
    pairs = []
    for k in range(per):
        for f in range(4):
            src = fields[f].at[pl.ds(first + k * count, count)]
            pairs.append((src, out.at[:, pl.ds((4 * k + f) * rows, rows), :]))
    copy_all(pairs, sems)


def pack(count, first, per, fields):
    _, rows, cols = fields[0].shape
    shape = (count, 4 * per * rows, cols)
    return pl.pallas_call(
        functools.partial(pack_body, first, per, rows),
        in_specs=[pl.BlockSpec(memory_space=pl.ANY)] * 4,
        out_specs=pl.BlockSpec(memory_space=pltpu.VMEM),
        out_shape=jax.ShapeDtypeStruct(shape, jnp.float32),
        scratch_shapes=[pltpu.SemaphoreType.DMA((4 * per,))],
        compiler_params=pltpu.CompilerParams(vmem_limit_bytes=32 * 1024 * 1024),
        cost_estimate=pl.CostEstimate(flops=0, bytes_accessed=8 * math.prod(shape), transcendentals=0),
    )(*fields)


def place_body(first, per, rows, *refs):
    got, outs, sems = refs[0], refs[-5:-1], refs[-1]
    count = got.shape[0]
    pairs = []
    for k in range(per):
        for f in range(4):
            src = got.at[:, pl.ds((4 * k + f) * rows, rows), :]
            pairs.append((src, outs[f].at[pl.ds(first + k * count, count)]))
    copy_all(pairs, sems)


def place(first, per, got, earlier, shape):
    return pl.pallas_call(
        functools.partial(place_body, first, per, shape[1]),
        in_specs=[pl.BlockSpec(memory_space=pltpu.VMEM)] + [pl.BlockSpec(memory_space=pl.ANY)] * len(earlier),
        out_specs=[pl.BlockSpec(memory_space=pl.ANY)] * 4,
        out_shape=[jax.ShapeDtypeStruct(shape, jnp.float32)] * 4,
        scratch_shapes=[pltpu.SemaphoreType.DMA((4 * per,))],
        input_output_aliases={1 + f: f for f in range(4)} if earlier else {},
        compiler_params=pltpu.CompilerParams(vmem_limit_bytes=32 * 1024 * 1024),
        cost_estimate=pl.CostEstimate(flops=0, bytes_accessed=8 * got.size, transcendentals=0),
    )(got, *earlier)


def lat_shift(x, amount, edge):
    size = x.shape[0]
    place = lax.broadcasted_iota(jnp.int32, x.shape, 0)
    at = size - 1 if amount < 0 else 0
    return jnp.where(place == at, edge, pltpu.roll(x, amount % size, 0))


def tend_body(count, rows, cols, dlon, dlat, where_ref, geo_ref, got_ref, south_ref, north_ref, *refs):
    tend_ref, even_ref, odd_ref = refs
    blocks = [got_ref.at[r] for r in range(count)]
    is_first, is_last = where_ref[0] == 1, where_ref[1] == 1
    geo = geo_ref[...]
    cs, cn = geo[:, 1:2], geo[:, 2:3]
    fs, fn, spin0, inv = geo[0:1, 3:4], geo[:, 4:5], geo[:, 5:6], geo[:, 6:7]
    wide = cols + 2 * LANES
    signs = (-1.0, -1.0, 1.0, 1.0)

    def mid(x):
        return x[:, LANES : LANES + cols]

    def east_of(x):
        return pltpu.roll(x, wide - 1, 1)

    def west_of(x):
        return pltpu.roll(x, 1, 1)

    for r in range(count):
        prev, here, nxt = blocks[r - 1], blocks[r], blocks[(r + 1) % count]
        across = blocks[(r + count // 2) % count]
        ext = []
        south, north = [], []
        for f in range(4):
            part = slice(f * rows, (f + 1) * rows)
            ext.append(jnp.concatenate([prev[part, cols - LANES :], here[part, :], nxt[part, :LANES]], axis=1))
            low, high = f * rows, (f + 1) * rows - 1
            south.append(jnp.where(is_first, signs[f] * across[low : low + 1, :], south_ref[r, 0, f : f + 1, :]))
            north.append(jnp.where(is_last, signs[f] * across[high : high + 1, :], north_ref[r, 0, f : f + 1, :]))
        ux, vx, px, hx = ext
        heat_x = px * hx
        energy_x = 0.5 * (ux * ux + vx * vx) + heat_x
        u, v, p, heat, energy = mid(ux), mid(vx), mid(px), mid(heat_x), mid(energy_x)
        out = slice(r * cols, (r + 1) * cols)

        zeta = (mid(east_of(vx)) - mid(west_of(vx))) * (0.5 / dlon)
        zeta -= (cn * lat_shift(u, -1, north[0]) - cs * lat_shift(u, 1, south[0])) * (0.5 / dlat)
        absolute = spin0 + zeta * inv
        edges = [0.5 * (q[0] * q[0] + q[1] * q[1]) + q[2] * q[3] for q in (south, north)]
        de_x = mid(east_of(energy_x)) - mid(west_of(energy_x))
        de_y = lat_shift(energy, -1, edges[1]) - lat_shift(energy, 1, edges[0])
        tend_ref[0:rows, out] = absolute * v - de_x * ((0.5 / dlon) * inv)
        tend_ref[rows : 2 * rows, out] = -absolute * u - de_y * (0.5 / dlat)

        a = 0.5 * (ux + east_of(ux))
        ap, am = jnp.maximum(a, 0.0), jnp.minimum(a, 0.0)
        flow_x = ap * px + am * east_of(px)
        hot_x = ap * heat_x + am * east_of(heat_x)
        b = 0.5 * (v + lat_shift(v, -1, north[1]))
        bp, bm = fn * jnp.maximum(b, 0.0), fn * jnp.minimum(b, 0.0)
        flow_y = bp * p + bm * lat_shift(p, -1, north[2])
        hot_y = bp * heat + bm * lat_shift(heat, -1, north[2] * north[3])
        b0 = 0.5 * (south[1] + v[0:1, :])
        bp0, bm0 = fs * jnp.maximum(b0, 0.0), fs * jnp.minimum(b0, 0.0)
        flow_y0 = bp0 * south[2] + bm0 * p[0:1, :]
        hot_y0 = bp0 * (south[2] * south[3]) + bm0 * heat[0:1, :]
        tend_ref[2 * rows : 3 * rows, out] = -inv * (
            (mid(flow_x) - mid(west_of(flow_x))) * (1.0 / dlon) + (flow_y - lat_shift(flow_y, 1, flow_y0)) * (1.0 / dlat)
        )
        tend_ref[3 * rows : 4 * rows, out] = -inv * (
            (mid(hot_x) - mid(west_of(hot_x))) * (1.0 / dlon) + (hot_y - lat_shift(hot_y, 1, hot_y0)) * (1.0 / dlat)
        )
    half = count * cols // 2
    for r in range(count // 2):
        near = tend_ref[:, r * cols : (r + 1) * cols]
        far = tend_ref[:, half + r * cols : half + (r + 1) * cols]
        even_ref[:, r * cols : (r + 1) * cols] = near + far
        odd_ref[:, r * cols : (r + 1) * cols] = near - far


def tendencies(rows, dlon, dlat, ends, geo, got, south, north):
    count, height, cols = got.shape
    full = count * cols
    high = 4 * rows
    halo = pl.BlockSpec((count, 1, 4, cols), lambda k: (0, k, 0, 0))
    return pl.pallas_call(
        functools.partial(tend_body, count, rows, cols, dlon, dlat),
        grid=(height // high,),
        in_specs=[
            pl.BlockSpec(memory_space=pltpu.SMEM),
            pl.BlockSpec((rows, 8), lambda k: (0, 0)),
            pl.BlockSpec((count, high, cols), lambda k: (0, k, 0)),
            halo,
            halo,
        ],
        out_specs=[
            pl.BlockSpec((high, full), lambda k: (k, 0)),
            pl.BlockSpec((high, full // 2), lambda k: (k, 0)),
            pl.BlockSpec((high, full // 2), lambda k: (k, 0)),
        ],
        out_shape=[
            jax.ShapeDtypeStruct((height, full), jnp.float32),
            jax.ShapeDtypeStruct((height, full // 2), jnp.float32),
            jax.ShapeDtypeStruct((height, full // 2), jnp.float32),
        ],
        compiler_params=pltpu.CompilerParams(vmem_limit_bytes=32 * 1024 * 1024),
        cost_estimate=pl.CostEstimate(flops=40 * height * full, bytes_accessed=12 * height * full, transcendentals=0),
    )(ends, geo, got, south, north)


def update_body(count, rows, cols, step_size, listed_ref, tend_ref, even_ref, odd_ref, got_ref, out_ref):
    listed = listed_ref[...] > 0
    half = count // 2
    for r in range(count):
        src = slice((r % half) * cols, (r % half + 1) * cols)
        for f in range(4):
            part = slice(f * rows, (f + 1) * rows)
            if r < half:
                smooth = even_ref[part, src] + odd_ref[part, src]
            else:
                smooth = even_ref[part, src] - odd_ref[part, src]
            chosen = jnp.where(listed, smooth, tend_ref[part, r * cols : (r + 1) * cols])
            base = got_ref[r, part, :]
            if f == 3:
                base = base * got_ref[r, 2 * rows : 3 * rows, :]
            out_ref[r, part, :] = base + step_size * chosen


def updated(rows, step_size, listed, tend, even, odd, got):
    count, height, cols = got.shape
    high = 4 * rows
    circles = pl.BlockSpec((count, high, cols), lambda k: (0, k, 0))
    flat = lambda width: pl.BlockSpec((high, width), lambda k: (k, 0))
    return pl.pallas_call(
        functools.partial(update_body, count, rows, cols, step_size),
        grid=(height // high,),
        in_specs=[
            pl.BlockSpec((rows, 1), lambda k: (0, 0)),
            flat(count * cols),
            flat(count * cols // 2),
            flat(count * cols // 2),
            circles,
        ],
        out_specs=circles,
        out_shape=jax.ShapeDtypeStruct(got.shape, jnp.float32),
        compiler_params=pltpu.CompilerParams(vmem_limit_bytes=32 * 1024 * 1024),
        cost_estimate=pl.CostEstimate(flops=4 * got.size, bytes_accessed=16 * got.size, transcendentals=0),
    )(listed, tend, even, odd, got)


def per_device(u_wind, v_wind, thickness, theta, polar_rows, cutoffs):
    levels, rows, cols = u_wind.shape
    lat_count = lax.axis_size("lat")
    count = lax.axis_size("lon")
    lat_place = lax.axis_index("lat")
    total_rows = rows * lat_count
    total_cols = cols * count
    dlon = 2.0 * math.pi / total_cols
    dlat = math.pi / total_rows
    step_size = 0.25 * dlon
    first_row = lat_place * rows
    fields = (u_wind, v_wind, thickness, theta)
    spread = levels // count
    chunks = [(0, 1), (count, spread - 1)]

    def exchanged(x):
        return lax.all_to_all(x, "lon", 0, 0, tiled=True)

    geo = lax.dynamic_slice_in_dim(jnp.asarray(geometry(total_rows)), first_row, rows, 0)
    own = first_row + jnp.arange(rows)
    listed = jnp.any(polar_rows.reshape(-1)[None, :] == own[:, None], axis=1)[:, None].astype(jnp.int32)
    limit = lax.dynamic_slice_in_dim(cutoffs, first_row, rows, 0)
    ends = jnp.stack([lat_place == 0, lat_place == lat_count - 1]).astype(jnp.int32)
    tables = [jnp.asarray(t) for t in fourier_tables(total_cols)]
    weights = []
    for odd in (0, 1):
        wave = 2 * jnp.arange(KHALF) + odd
        w = jnp.where(wave[None, :] == 0, 1.0, jnp.where(wave[None, :] <= limit[:, None], 2.0, 0.0)) / total_cols
        weights.append(jnp.concatenate([w, w], axis=1))

    circles = [exchanged(pack(count, first, per, fields)) for first, per in chunks]
    high = lax.Precision.HIGH
    done = ()
    for got, (first, per) in zip(circles, chunks):
        split = got.reshape(count, per, 4, rows, cols)
        south = lax.ppermute(split[:, :, :, rows - 1], "lat", [(i, i + 1) for i in range(lat_count - 1)])
        north = lax.ppermute(split[:, :, :, 0], "lat", [(i + 1, i) for i in range(lat_count - 1)])
        tend, *sides = tendencies(rows, dlon, dlat, ends, geo, got, south, north)
        smooth = []
        for x, table, weight in zip(sides, tables, weights):
            spectrum = jnp.dot(x, table, precision=high, preferred_element_type=jnp.float32)
            spectrum = spectrum * jnp.tile(weight, (4 * per, 1))
            smooth.append(jnp.dot(spectrum, table.T, precision=high, preferred_element_type=jnp.float32))
        fresh = exchanged(updated(rows, step_size, listed, tend, *smooth, got))
        done = place(first, per, fresh, done, (levels, rows, cols))
    return tuple(done)


def solution(mesh):
    field = P(None, "lat", "lon")
    return jax.shard_map(
        per_device,
        mesh=mesh,
        in_specs=(field, field, field, field, P(), P()),
        out_specs=(field, field, field, field),
        check_vma=False,
    )
```

```python
import functools
import math

import jax
import jax.numpy as jnp
import numpy as np
from jax import lax
from jax.experimental import pallas as pl
from jax.experimental.pallas import tpu as pltpu
from jax.sharding import PartitionSpec as P

OMEGA = 30.0
SECTORS = 8
REAL_Q = 64
FULL_Q = 128
SHIFT_Q = 52
LANES = 128


def geometry(total_rows):
    row = np.arange(-1, total_rows + 1)
    dist = np.maximum(np.minimum(row, total_rows - 1 - row), 0)
    cos_row = np.sin(np.pi * (dist + 0.5) / total_rows)
    face = np.arange(total_rows + 1)
    cos_face = np.sin(np.pi * np.minimum(face, total_rows - face) / total_rows)
    spin = -2.0 * OMEGA * np.cos(np.pi * (np.arange(total_rows) + 0.5) / total_rows)
    table = np.zeros((total_rows, 8))
    table[:, 0] = cos_row[1:-1]
    table[:, 1] = cos_row[:-2]
    table[:, 2] = cos_row[2:]
    table[:, 3] = cos_face[:-1]
    table[:, 4] = cos_face[1:]
    table[:, 5] = spin
    table[:, 6] = 1.0 / cos_row[1:-1]
    return table.astype(np.float32)


def split(x):
    high = x.astype(jnp.bfloat16)
    return high, (x - high.astype(jnp.float32)).astype(jnp.bfloat16)


def fourier_tables(total):
    column = np.arange(total // SECTORS)

    def angle(wave):
        return (column[:, None] * wave[None, :] % total) * (2.0 * np.pi / total)

    real, full = [], []
    for r in (0, 4):
        theta = angle(SECTORS * np.arange(REAL_Q) + r)
        real.append(np.concatenate([np.cos(theta), -np.sin(theta)], axis=1))
    for r in (1, 2, 3):
        theta = angle(SECTORS * (np.arange(FULL_Q) - SHIFT_Q) + r)
        cos, sin = np.cos(theta), np.sin(theta)
        full.append(np.block([[cos, -sin], [sin, cos]]))

    def halves(table):
        table = table.astype(np.float32)
        high = table.astype(jnp.bfloat16)
        return np.stack([high, (table - high.astype(np.float32)).astype(jnp.bfloat16)], axis=1)

    real, full = np.stack(real), np.stack(full)
    tables = (real, full, real.transpose(0, 2, 1), full.transpose(0, 2, 1))
    return [jnp.asarray(halves(t)) for t in tables]


def copy_all(pairs, sems):
    copies = [pltpu.make_async_copy(src, dst, sems.at[i]) for i, (src, dst) in enumerate(pairs)]
    for copy in copies:
        copy.start()
    for copy in copies:
        copy.wait()


def pack_body(count, per, rows, *refs):
    fields, out, sems = refs[:4], refs[4], refs[5]
    pairs = []
    for d in range(count):
        for k in range(per):
            for f in range(4):
                pairs.append((fields[f].at[d * per + k], out.at[d, pl.ds((4 * k + f) * rows, rows), :]))
    copy_all(pairs, sems)


def pack(count, fields):
    levels, rows, cols = fields[0].shape
    shape = (count, 4 * (levels // count) * rows, cols)
    return pl.pallas_call(
        functools.partial(pack_body, count, levels // count, rows),
        in_specs=[pl.BlockSpec(memory_space=pl.ANY)] * 4,
        out_specs=pl.BlockSpec(memory_space=pltpu.VMEM),
        out_shape=jax.ShapeDtypeStruct(shape, jnp.float32),
        scratch_shapes=[pltpu.SemaphoreType.DMA((4 * levels,))],
        compiler_params=pltpu.CompilerParams(vmem_limit_bytes=56 * 1024 * 1024),
        cost_estimate=pl.CostEstimate(flops=0, bytes_accessed=8 * math.prod(shape), transcendentals=0),
    )(*fields)


def place_body(count, per, rows, *refs):
    got, outs, sems = refs[0], refs[1:5], refs[5]
    pairs = []
    for d in range(count):
        for k in range(per):
            for f in range(4):
                pairs.append((got.at[d, pl.ds((4 * k + f) * rows, rows), :], outs[f].at[d * per + k]))
    copy_all(pairs, sems)


def place(got, shape):
    count = got.shape[0]
    return pl.pallas_call(
        functools.partial(place_body, count, shape[0] // count, shape[1]),
        in_specs=[pl.BlockSpec(memory_space=pltpu.VMEM)],
        out_specs=[pl.BlockSpec(memory_space=pl.ANY)] * 4,
        out_shape=[jax.ShapeDtypeStruct(shape, jnp.float32)] * 4,
        scratch_shapes=[pltpu.SemaphoreType.DMA((4 * shape[0],))],
        compiler_params=pltpu.CompilerParams(vmem_limit_bytes=32 * 1024 * 1024),
        cost_estimate=pl.CostEstimate(flops=0, bytes_accessed=8 * got.size, transcendentals=0),
    )(got)


def lat_shift(x, amount, edge):
    size = x.shape[0]
    place = lax.broadcasted_iota(jnp.int32, x.shape, 0)
    at = size - 1 if amount < 0 else 0
    return jnp.where(place == at, edge, pltpu.roll(x, amount % size, 0))


def level_tendencies(level, count, rows, cols, dlon, dlat, where_ref, geo_ref, got_ref, halo_ref, tend_ref):
    high = 4 * rows
    start = pl.multiple_of(level * high, high)
    halo_start = pl.multiple_of(level * 8, 8)
    blocks = [got_ref.at[r, pl.ds(start, high), :] for r in range(count)]
    halos = [halo_ref[r, pl.ds(halo_start, 8), :] for r in range(count)]
    is_first, is_last = where_ref[0] == 1, where_ref[1] == 1
    geo = geo_ref[...]
    cs, cn = geo[:, 1:2], geo[:, 2:3]
    fs, fn, spin0, inv = geo[0:1, 3:4], geo[:, 4:5], geo[:, 5:6], geo[:, 6:7]
    wide = cols + 2 * LANES
    signs = (-1.0, -1.0, 1.0, 1.0)

    def mid(x):
        return x[:, LANES : LANES + cols]

    def east_of(x):
        return pltpu.roll(x, wide - 1, 1)

    def west_of(x):
        return pltpu.roll(x, 1, 1)

    for r in range(count):
        prev, here, nxt = blocks[r - 1], blocks[r], blocks[(r + 1) % count]
        across = blocks[(r + count // 2) % count]
        ext = []
        south, north = [], []
        for f in range(4):
            part = slice(f * rows, (f + 1) * rows)
            ext.append(jnp.concatenate([prev[part, cols - LANES :], here[part, :], nxt[part, :LANES]], axis=1))
            low, top = f * rows, (f + 1) * rows - 1
            south.append(jnp.where(is_first, signs[f] * across[low : low + 1, :], halos[r][f : f + 1, :]))
            north.append(jnp.where(is_last, signs[f] * across[top : top + 1, :], halos[r][4 + f : 5 + f, :]))
        ux, vx, px, hx = ext
        heat_x = px * hx
        energy_x = 0.5 * (ux * ux + vx * vx) + heat_x
        u, v, p, heat, energy = mid(ux), mid(vx), mid(px), mid(heat_x), mid(energy_x)
        out = tend_ref.at[r, pl.ds(start, high), :]

        zeta = (mid(east_of(vx)) - mid(west_of(vx))) * (0.5 / dlon)
        zeta -= (cn * lat_shift(u, -1, north[0]) - cs * lat_shift(u, 1, south[0])) * (0.5 / dlat)
        absolute = spin0 + zeta * inv
        edges = [0.5 * (q[0] * q[0] + q[1] * q[1]) + q[2] * q[3] for q in (south, north)]
        de_x = mid(east_of(energy_x)) - mid(west_of(energy_x))
        de_y = lat_shift(energy, -1, edges[1]) - lat_shift(energy, 1, edges[0])
        out[0:rows, :] = absolute * v - de_x * ((0.5 / dlon) * inv)
        out[rows : 2 * rows, :] = -absolute * u - de_y * (0.5 / dlat)

        a = 0.5 * (ux + east_of(ux))
        ap, am = jnp.maximum(a, 0.0), jnp.minimum(a, 0.0)
        flow_x = ap * px + am * east_of(px)
        hot_x = ap * heat_x + am * east_of(heat_x)
        b = 0.5 * (v + lat_shift(v, -1, north[1]))
        bp, bm = fn * jnp.maximum(b, 0.0), fn * jnp.minimum(b, 0.0)
        flow_y = bp * p + bm * lat_shift(p, -1, north[2])
        hot_y = bp * heat + bm * lat_shift(heat, -1, north[2] * north[3])
        b0 = 0.5 * (south[1] + v[0:1, :])
        bp0, bm0 = fs * jnp.maximum(b0, 0.0), fs * jnp.minimum(b0, 0.0)
        flow_y0 = bp0 * south[2] + bm0 * p[0:1, :]
        hot_y0 = bp0 * (south[2] * south[3]) + bm0 * heat[0:1, :]
        out[2 * rows : 3 * rows, :] = -inv * (
            (mid(flow_x) - mid(west_of(flow_x))) * (1.0 / dlon) + (flow_y - lat_shift(flow_y, 1, flow_y0)) * (1.0 / dlat)
        )
        out[3 * rows : 4 * rows, :] = -inv * (
            (mid(hot_x) - mid(west_of(hot_x))) * (1.0 / dlon) + (hot_y - lat_shift(hot_y, 1, hot_y0)) * (1.0 / dlat)
        )


def butterfly(rows_at, cols, tend_ref, high_ref, low_ref):
    x = [tend_ref[b, rows_at, :] for b in range(SECTORS)]
    s = [x[b] + x[b + 4] for b in range(4)]
    d = [x[b] - x[b + 4] for b in range(4)]
    c = math.sqrt(0.5)
    even, odd = s[0] + s[2], s[1] + s[3]
    plus, minus = c * (d[1] + d[3]), c * (d[1] - d[3])
    parts = (even + odd, even - odd, d[0] + minus, -d[2] - plus, s[0] - s[2], s[3] - s[1], d[0] - minus, d[2] - plus)
    for i, part in enumerate(parts):
        at = slice(i * cols, (i + 1) * cols)
        high_ref[rows_at, at], low_ref[rows_at, at] = split(part)


def product(high, low, table_ref, *index):
    big, small = table_ref[(*index, 0)], table_ref[(*index, 1)]
    total = jnp.dot(high, big, preferred_element_type=jnp.float32)
    total += jnp.dot(low, big, preferred_element_type=jnp.float32)
    return total + jnp.dot(high, small, preferred_element_type=jnp.float32)


def truncate(total, cols, limit_ref, tables, high_ref, low_ref, wave_ref):
    real_ref, full_ref, real_back_ref, full_back_ref = tables
    limit = limit_ref[...]
    for i, r in enumerate((0, 4, 1, 2, 3)):
        if i < 2:
            at, half = slice(i * cols, (i + 1) * cols), REAL_Q
            ahead, back, place = real_ref, real_back_ref, i
        else:
            at, half = slice((2 * i - 2) * cols, 2 * i * cols), FULL_Q
            ahead, back, place = full_ref, full_back_ref, i - 2
        spectrum = product(high_ref[:, at], low_ref[:, at], ahead, place)
        lane = lax.broadcasted_iota(jnp.int32, (1, 2 * half), 1)
        q = jnp.where(lane >= half, lane - half, lane) - (0 if i < 2 else SHIFT_Q)
        k = jnp.abs(SECTORS * q + r)
        factor = jnp.where(k <= limit, jnp.where(k == 0, 1.0 / total, 2.0 / total), 0.0)
        wave_ref[:, at] = product(*split(spectrum * factor), back, place)


def update(level, rows, cols, step_size, listed_ref, got_ref, tend_ref, wave_ref, out_ref):
    c = math.sqrt(0.5)
    high = 4 * rows
    for f in range(4):
        for j in range(0, rows, 8):
            at = pl.ds(pl.multiple_of(level * high + f * rows + j, 8), 8)
            w0, w4, a1, b1, a2, b2, a3, b3 = [wave_ref[at, i * cols : (i + 1) * cols] for i in range(SECTORS)]
            near, far = w0 + w4, w0 - w4
            even = (near + a2, far - b2, near - a2, far + b2)
            odd = (a1 + a3, c * ((a1 - b1) - (a3 + b3)), b3 - b1, c * ((a3 - b3) - (a1 + b1)))
            listed = listed_ref[j : j + 8, :] > 0
            for b in range(SECTORS):
                smooth = even[b % 4] + odd[b % 4] if b < 4 else even[b % 4] - odd[b % 4]
                base = got_ref[b, at, :]
                if f == 3:
                    base = base * got_ref[b, pl.ds(pl.multiple_of(level * high + 2 * rows + j, 8), 8), :]
                out_ref[b, at, :] = base + step_size * jnp.where(listed, smooth, tend_ref[b, at, :])


def step_body(per, rows, cols, dlon, dlat, step_size, where_ref, geo_ref, limit_ref, listed_ref, got_ref, *refs):
    tables, halos = refs[:4], refs[4 : 4 + SECTORS]
    out_ref, tend_ref, high_ref, low_ref, wave_ref, halo_ref = refs[4 + SECTORS :]
    high = 4 * rows
    for r in range(SECTORS):
        halo_ref[lax.rem(where_ref[2] + r, SECTORS)] = halos[r][0]

    @pl.loop(0, per)
    def _(level):
        level_tendencies(level, SECTORS, rows, cols, dlon, dlat, where_ref, geo_ref, got_ref, halo_ref, tend_ref)

    @pl.loop(0, per * high // 16)
    def _(group):
        butterfly(pl.ds(pl.multiple_of(group * 16, 16), 16), cols, tend_ref, high_ref, low_ref)

    truncate(SECTORS * cols, cols, limit_ref, tables, high_ref, low_ref, wave_ref)

    @pl.loop(0, per)
    def _(level):
        update(level, rows, cols, step_size, listed_ref, got_ref, tend_ref, wave_ref, out_ref)


def stepped(rows, dlon, dlat, step_size, where, geo, limit, listed, got, halos, tables):
    count, height, cols = got.shape
    inside = pl.BlockSpec(memory_space=pltpu.VMEM)
    full = count * cols
    return pl.pallas_call(
        functools.partial(step_body, height // (4 * rows), rows, cols, dlon, dlat, step_size),
        in_specs=[pl.BlockSpec(memory_space=pltpu.SMEM)] + [inside] * (8 + count),
        out_specs=inside,
        out_shape=jax.ShapeDtypeStruct(got.shape, jnp.float32),
        scratch_shapes=[
            pltpu.VMEM(got.shape, jnp.float32),
            pltpu.VMEM((height, full), jnp.bfloat16),
            pltpu.VMEM((height, full), jnp.bfloat16),
            pltpu.VMEM((height, full), jnp.float32),
            pltpu.VMEM((count, height // (4 * rows) * 8, cols), jnp.float32),
        ],
        compiler_params=pltpu.CompilerParams(vmem_limit_bytes=48 * 1024 * 1024),
        cost_estimate=pl.CostEstimate(flops=8 * 1024 * 1024 * height, bytes_accessed=24 * height * full, transcendentals=0),
    )(where, geo, limit, listed, got, *tables, *halos)


def per_device(u_wind, v_wind, thickness, theta, polar_rows, cutoffs):
    levels, rows, cols = u_wind.shape
    lat_count = lax.axis_size("lat")
    count = lax.axis_size("lon")
    lat_place = lax.axis_index("lat")
    me = lax.axis_index("lon")
    total_rows = rows * lat_count
    total_cols = cols * count
    dlon = 2.0 * math.pi / total_cols
    dlat = math.pi / total_rows
    step_size = 0.25 * dlon
    first_row = lat_place * rows
    fields = (u_wind, v_wind, thickness, theta)
    per = levels // count

    got = lax.all_to_all(pack(count, fields), "lon", 0, 0, tiled=True)

    low_rows = jnp.stack([f[:, 0, :] for f in fields], axis=1)
    high_rows = jnp.stack([f[:, rows - 1, :] for f in fields], axis=1)
    south = lax.ppermute(high_rows, "lat", [(i, i + 1) for i in range(lat_count - 1)])
    north = lax.ppermute(low_rows, "lat", [(i + 1, i) for i in range(lat_count - 1)])
    halo = jnp.concatenate([south, north], axis=1).reshape(count, 8 * per, cols)
    turned = [lax.dynamic_slice_in_dim(halo, lax.rem(me + step, count), 1, 0) for step in range(count)]
    for step in range(1, count):
        turned[step] = lax.ppermute(turned[step], "lon", [(i, (i + step) % count) for i in range(count)])
    halos = [turned[(count - r) % count] for r in range(count)]

    geo = lax.dynamic_slice_in_dim(jnp.asarray(geometry(total_rows)), first_row, rows, 0)
    own = first_row + jnp.arange(rows)
    listed = jnp.any(polar_rows.reshape(-1)[None, :] == own[:, None], axis=1)[:, None].astype(jnp.int32)
    limit = jnp.tile(lax.dynamic_slice_in_dim(cutoffs, first_row, rows, 0), 4 * per)[:, None]
    where = jnp.stack([lat_place == 0, lat_place == lat_count - 1, me]).astype(jnp.int32)
    tables = fourier_tables(total_cols)
    fresh = stepped(rows, dlon, dlat, step_size, where, geo, limit, listed, got, halos, tables)
    return tuple(place(lax.all_to_all(fresh, "lon", 0, 0, tiled=True), u_wind.shape))


def solution(mesh):
    field = P(None, "lat", "lon")
    return jax.shard_map(
        per_device,
        mesh=mesh,
        in_specs=(field, field, field, field, P(), P()),
        out_specs=(field, field, field, field),
        check_vma=False,
    )
```

```python
import functools
import math

import jax
import jax.numpy as jnp
import numpy as np
from jax import lax
from jax.experimental import pallas as pl
from jax.experimental.pallas import tpu as pltpu
from jax.sharding import PartitionSpec as P

OMEGA = 30.0
SECTORS = 8
REAL_Q = 64
FULL_Q = 128
SHIFT_Q = 52
LANES = 128


def geometry(total_rows):
    row = np.arange(-1, total_rows + 1)
    dist = np.maximum(np.minimum(row, total_rows - 1 - row), 0)
    cos_row = np.sin(np.pi * (dist + 0.5) / total_rows)
    face = np.arange(total_rows + 1)
    cos_face = np.sin(np.pi * np.minimum(face, total_rows - face) / total_rows)
    spin = -2.0 * OMEGA * np.cos(np.pi * (np.arange(total_rows) + 0.5) / total_rows)
    table = np.zeros((total_rows, 8))
    table[:, 0] = cos_row[1:-1]
    table[:, 1] = cos_row[:-2]
    table[:, 2] = cos_row[2:]
    table[:, 3] = cos_face[:-1]
    table[:, 4] = cos_face[1:]
    table[:, 5] = spin
    table[:, 6] = 1.0 / cos_row[1:-1]
    return table.astype(np.float32)


def split(x):
    high = x.astype(jnp.bfloat16)
    return high, (x - high.astype(jnp.float32)).astype(jnp.bfloat16)


def fourier_tables(total):
    column = np.arange(total // SECTORS)

    def angle(wave):
        return (column[:, None] * wave[None, :] % total) * (2.0 * np.pi / total)

    real, full = [], []
    for r in (0, 4):
        theta = angle(SECTORS * np.arange(REAL_Q) + r)
        real.append(np.concatenate([np.cos(theta), -np.sin(theta)], axis=1))
    for r in (1, 2, 3):
        theta = angle(SECTORS * (np.arange(FULL_Q) - SHIFT_Q) + r)
        cos, sin = np.cos(theta), np.sin(theta)
        full.append(np.block([[cos, -sin], [sin, cos]]))

    def halves(table):
        table = table.astype(np.float32)
        high = table.astype(jnp.bfloat16)
        return np.stack([high, (table - high.astype(np.float32)).astype(jnp.bfloat16)], axis=1)

    real, full = np.stack(real), np.stack(full)
    tables = (real, full, real.transpose(0, 2, 1), full.transpose(0, 2, 1))
    return [jnp.asarray(halves(t)) for t in tables]


def copy_all(pairs, sems):
    copies = [pltpu.make_async_copy(src, dst, sems.at[i]) for i, (src, dst) in enumerate(pairs)]
    for copy in copies:
        copy.start()
    for copy in copies:
        copy.wait()


def pack_body(count, per, rows, *refs):
    fields, out, held, arrive, leave = refs[:4], *refs[4:]
    comes, goes = [], []
    for d in range(count):
        for k in range(per):
            for f in range(4):
                at = pl.ds((4 * k + f) * rows, rows)
                i = len(comes)
                comes.append(pltpu.make_async_copy(fields[f].at[d * per + k], held.at[d, at, :], arrive.at[i]))
        goes.append(pltpu.make_async_copy(held.at[d], out.at[d], leave.at[d]))
    for copy in comes:
        copy.start()
    for d in range(count):
        for copy in comes[4 * per * d : 4 * per * (d + 1)]:
            copy.wait()
        goes[d].start()
    for copy in goes:
        copy.wait()


def pack(count, fields):
    levels, rows, cols = fields[0].shape
    shape = (count, 4 * (levels // count) * rows, cols)
    return pl.pallas_call(
        functools.partial(pack_body, count, levels // count, rows),
        in_specs=[pl.BlockSpec(memory_space=pl.ANY)] * 4,
        out_specs=pl.BlockSpec(memory_space=pl.ANY),
        out_shape=jax.ShapeDtypeStruct(shape, jnp.float32),
        scratch_shapes=[
            pltpu.VMEM(shape, jnp.float32),
            pltpu.SemaphoreType.DMA((4 * levels,)),
            pltpu.SemaphoreType.DMA((count,)),
        ],
        compiler_params=pltpu.CompilerParams(vmem_limit_bytes=56 * 1024 * 1024),
        cost_estimate=pl.CostEstimate(flops=0, bytes_accessed=8 * math.prod(shape), transcendentals=0),
    )(*fields)


def place_body(count, per, rows, *refs):
    got, outs, sems = refs[0], refs[1:5], refs[5]
    pairs = []
    for d in range(count):
        for k in range(per):
            for f in range(4):
                pairs.append((got.at[d, pl.ds((4 * k + f) * rows, rows), :], outs[f].at[d * per + k]))
    copy_all(pairs, sems)


def place(got, shape):
    count = got.shape[0]
    return pl.pallas_call(
        functools.partial(place_body, count, shape[0] // count, shape[1]),
        in_specs=[pl.BlockSpec(memory_space=pltpu.VMEM)],
        out_specs=[pl.BlockSpec(memory_space=pl.ANY)] * 4,
        out_shape=[jax.ShapeDtypeStruct(shape, jnp.float32)] * 4,
        scratch_shapes=[pltpu.SemaphoreType.DMA((4 * shape[0],))],
        compiler_params=pltpu.CompilerParams(vmem_limit_bytes=32 * 1024 * 1024),
        cost_estimate=pl.CostEstimate(flops=0, bytes_accessed=8 * got.size, transcendentals=0),
    )(got)


def lat_shift(x, amount, edge):
    size = x.shape[0]
    place = lax.broadcasted_iota(jnp.int32, x.shape, 0)
    at = size - 1 if amount < 0 else 0
    return jnp.where(place == at, edge, pltpu.roll(x, amount % size, 0))


def group_tendencies(level, first, size, span, rows, cols, dlon, dlat, place, geo_ref, got_ref, halo_refs, tend_ref, skip=0):
    start = pl.multiple_of(level * 4 * rows, 4 * rows)
    geo = geo_ref[pl.ds(pl.multiple_of(place * rows + first, 8), size), :]
    fs, fn, spin0, inv = geo[0:1, 3:4], geo[:, 4:5], geo[:, 5:6], geo[:, 6:7]
    to_east = (0.5 / dlon) * inv
    to_south, to_north = (0.5 / dlat) * (geo[:, 1:2] * inv), (0.5 / dlat) * (geo[:, 2:3] * inv)
    out_x, out_y = (-1.0 / dlon) * inv, (-1.0 / dlat) * inv
    wide = span * cols + 2 * LANES
    signs = (-1.0, -1.0, 1.0, 1.0)

    def mid(x):
        return x[:, LANES : LANES + span * cols]

    def east_of(x):
        return pltpu.roll(x, wide - 1, 1)

    def west_of(x):
        return pltpu.roll(x, 1, 1)

    def joined(parts):
        return parts[0] if len(parts) == 1 else jnp.concatenate(parts, axis=1)

    def edge_row(f, r, row, side, at_pole):
        if 0 <= row < rows:
            return got_ref[r, pl.ds(start + f * rows + row, 1), :]
        near = 0 if row < 0 else rows - 1
        across = got_ref[(r + SECTORS // 2) % SECTORS, pl.ds(start + f * rows + near, 1), :]
        return jnp.where(at_pole, signs[f] * across, halo_refs[side][r, level, f : f + 1, :])

    for base in range(0, SECTORS, span):
        sectors = range(base, base + span)
        ext, south, north = [], [], []
        for f in range(4):
            part = pl.ds(pl.multiple_of(start + f * rows + first, 8), size)
            ext.append(
                jnp.concatenate(
                    [got_ref[(base - 1) % SECTORS, part, cols - LANES :]]
                    + [got_ref[r, part, :] for r in sectors]
                    + [got_ref[(base + span) % SECTORS, part, :LANES]],
                    axis=1,
                )
            )
            south.append(joined([edge_row(f, r, first - 1, 0, place == 0) for r in sectors]))
            north.append(joined([edge_row(f, r, first + size, 1, place == lax.axis_size("lat") - 1) for r in sectors]))
        ux, vx, px, hx = ext
        heat_x = px * hx
        energy_x = 0.5 * (ux * ux + vx * vx) + heat_x
        u, v, p, heat, energy = mid(ux), mid(vx), mid(px), mid(heat_x), mid(energy_x)

        spin = spin0 + (mid(east_of(vx)) - mid(west_of(vx))) * to_east
        spin -= to_north * lat_shift(u, -1, north[0]) - to_south * lat_shift(u, 1, south[0])
        edges = [0.5 * (q[0] * q[0] + q[1] * q[1]) + q[2] * q[3] for q in (south, north)]
        de_x = mid(east_of(energy_x)) - mid(west_of(energy_x))
        de_y = lat_shift(energy, -1, edges[1]) - lat_shift(energy, 1, edges[0])
        u_t = spin * v - de_x * to_east
        v_t = de_y * (-0.5 / dlat) - spin * u

        a = 0.5 * (ux + east_of(ux))
        ap, am = jnp.maximum(a, 0.0), jnp.minimum(a, 0.0)
        flow_x = ap * px + am * east_of(px)
        hot_x = ap * heat_x + am * east_of(heat_x)
        b = (0.5 * fn) * (v + lat_shift(v, -1, north[1]))
        bp, bm = jnp.maximum(b, 0.0), jnp.minimum(b, 0.0)
        flow_y = bp * p + bm * lat_shift(p, -1, north[2])
        hot_y = bp * heat + bm * lat_shift(heat, -1, north[2] * north[3])
        b0 = (0.5 * fs) * (south[1] + v[0:1, :])
        bp0, bm0 = jnp.maximum(b0, 0.0), jnp.minimum(b0, 0.0)
        flow_y0 = bp0 * south[2] + bm0 * p[0:1, :]
        hot_y0 = bp0 * (south[2] * south[3]) + bm0 * heat[0:1, :]
        p_t = (mid(flow_x) - mid(west_of(flow_x))) * out_x + (flow_y - lat_shift(flow_y, 1, flow_y0)) * out_y
        h_t = (mid(hot_x) - mid(west_of(hot_x))) * out_x + (hot_y - lat_shift(hot_y, 1, hot_y0)) * out_y
        for f, value in enumerate((u_t, v_t, p_t, h_t)):
            kept = rows - 2 * skip
            part = pl.ds(pl.multiple_of(level * 4 * kept + f * kept + first - skip, 8), size)
            for i, r in enumerate(sectors):
                tend_ref[r, part, :] = value[:, i * cols : (i + 1) * cols]


def butterfly(rows_at, cols, tend_ref, high_ref, low_ref):
    x = [tend_ref[b, rows_at, :] for b in range(SECTORS)]
    s = [x[b] + x[b + 4] for b in range(4)]
    d = [x[b] - x[b + 4] for b in range(4)]
    c = math.sqrt(0.5)
    even, odd = s[0] + s[2], s[1] + s[3]
    plus, minus = c * (d[1] + d[3]), c * (d[1] - d[3])
    parts = (even + odd, even - odd, d[0] + minus, -d[2] - plus, s[0] - s[2], s[3] - s[1], d[0] - minus, d[2] - plus)
    for i, part in enumerate(parts):
        at = slice(i * cols, (i + 1) * cols)
        high_ref[rows_at, at], low_ref[rows_at, at] = split(part)


def product(high, low, table_ref, *index):
    big, small = table_ref[(*index, 0)], table_ref[(*index, 1)]
    total = jnp.dot(high, big, preferred_element_type=jnp.float32)
    total += jnp.dot(low, big, preferred_element_type=jnp.float32)
    return total + jnp.dot(high, small, preferred_element_type=jnp.float32)


def truncate(total, cols, limit, tables, high_ref, low_ref, wave_ref):
    real_ref, full_ref, real_back_ref, full_back_ref = tables
    for i, r in enumerate((0, 4, 1, 2, 3)):
        if i < 2:
            at, half = slice(i * cols, (i + 1) * cols), REAL_Q
            ahead, back, place = real_ref, real_back_ref, i
        else:
            at, half = slice((2 * i - 2) * cols, 2 * i * cols), FULL_Q
            ahead, back, place = full_ref, full_back_ref, i - 2
        spectrum = product(high_ref[:, at], low_ref[:, at], ahead, place)
        lane = lax.broadcasted_iota(jnp.int32, (1, 2 * half), 1)
        q = jnp.where(lane >= half, lane - half, lane) - (0 if i < 2 else SHIFT_Q)
        k = jnp.abs(SECTORS * q + r)
        factor = jnp.where(k <= limit, jnp.where(k == 0, 1.0 / total, 2.0 / total), 0.0)
        wave_ref[:, at] = product(*split(spectrum * factor), back, place)


def update(level, rows, cols, step_size, listed, got_ref, tend_ref, wave_ref, out_ref):
    c = math.sqrt(0.5)
    high = 4 * rows
    for f in range(4):
        for j in range(0, rows, 8):
            at = pl.ds(pl.multiple_of(level * high + f * rows + j, 8), 8)
            w0, w4, a1, b1, a2, b2, a3, b3 = [wave_ref[at, i * cols : (i + 1) * cols] for i in range(SECTORS)]
            near, far = w0 + w4, w0 - w4
            even = (near + a2, far - b2, near - a2, far + b2)
            odd = (a1 + a3, c * ((a1 - b1) - (a3 + b3)), b3 - b1, c * ((a3 - b3) - (a1 + b1)))
            chosen = listed[j : j + 8, :]
            for b in range(SECTORS):
                smooth = even[b % 4] + odd[b % 4] if b < 4 else even[b % 4] - odd[b % 4]
                base = got_ref[b, at, :]
                if f == 3:
                    base = base * got_ref[b, pl.ds(pl.multiple_of(level * high + 2 * rows + j, 8), 8), :]
                out_ref[b, at, :] = base + step_size * jnp.where(chosen, smooth, tend_ref[b, at, :])


def inner_body(per, rows, cols, dlon, dlat, geo_ref, got_ref, tend_ref):
    place = lax.axis_index("lat")

    @pl.loop(0, per)
    def _(level):
        for first in range(8, rows - 8, 8):
            group_tendencies(level, first, 8, 2, rows, cols, dlon, dlat, place, geo_ref, got_ref, None, tend_ref, 8)


def inner_tendencies(rows, dlon, dlat, geo, got):
    inside = pl.BlockSpec(memory_space=pltpu.VMEM)
    return pl.pallas_call(
        functools.partial(inner_body, got.shape[1] // (4 * rows), rows, got.shape[2], dlon, dlat),
        in_specs=[inside, inside],
        out_specs=inside,
        out_shape=jax.ShapeDtypeStruct((got.shape[0], got.shape[1] // rows * (rows - 16), got.shape[2]), jnp.float32),
        compiler_params=pltpu.CompilerParams(vmem_limit_bytes=12 * 1024 * 1024),
        cost_estimate=pl.CostEstimate(flops=40 * got.size, bytes_accessed=6 * got.size, transcendentals=0),
    )(geo, got)


def step_body(per, rows, cols, dlon, dlat, step_size, geo_ref, polar_ref, cutoff_ref, got_ref, tend_ref, south_ref, north_ref, *refs):
    tables = refs[:4]
    out_ref, edge_ref, high_ref, low_ref, wave_ref = refs[4:]
    high = 4 * rows
    halos = (south_ref, north_ref)
    place = lax.axis_index("lat")
    total = rows * lax.axis_size("lat")
    edge = jnp.sum((polar_ref[...] < total // 2).astype(jnp.int32))
    own = place * rows + lax.broadcasted_iota(jnp.int32, (rows, 1), 0)
    listed = (own < edge) | (own >= total // 2 + edge)
    bands = LANES // rows
    cut = cutoff_ref[pl.ds(place // bands, 1), :]
    lane = lax.broadcasted_iota(jnp.int32, (rows, LANES), 1)
    mine = lane == lax.rem(place, bands) * rows + lax.broadcasted_iota(jnp.int32, (rows, LANES), 0)
    limit = jnp.sum(jnp.where(mine, cut, 0), axis=1, keepdims=True)
    limit = jnp.concatenate([limit] * (4 * per), axis=0)

    @pl.loop(0, per)
    def _(level):
        for first in (0, rows - 8):
            group_tendencies(level, first, 8, 2, rows, cols, dlon, dlat, place, geo_ref, got_ref, halos, edge_ref)
        for f in range(4):
            part = pl.ds(pl.multiple_of(level * high + f * rows + 8, 8), rows - 16)
            kept = pl.ds(pl.multiple_of((level * 4 + f) * (rows - 16), 8), rows - 16)
            for r in range(SECTORS):
                edge_ref[r, part, :] = tend_ref[r, kept, :]

    @pl.loop(0, per * high // 16)
    def _(group):
        butterfly(pl.ds(pl.multiple_of(group * 16, 16), 16), cols, edge_ref, high_ref, low_ref)

    truncate(SECTORS * cols, cols, limit, tables, high_ref, low_ref, wave_ref)

    @pl.loop(0, per)
    def _(level):
        update(level, rows, cols, step_size, listed, got_ref, edge_ref, wave_ref, out_ref)


def stepped(rows, dlon, dlat, step_size, geo, polar_rows, cutoffs, got, tend, south, north, tables):
    count, height, cols = got.shape
    inside = pl.BlockSpec(memory_space=pltpu.VMEM)
    full = count * cols
    return pl.pallas_call(
        functools.partial(step_body, height // (4 * rows), rows, cols, dlon, dlat, step_size),
        in_specs=[inside] * 11,
        out_specs=inside,
        out_shape=jax.ShapeDtypeStruct(got.shape, jnp.float32),
        scratch_shapes=[
            pltpu.VMEM(got.shape, jnp.float32),
            pltpu.VMEM((height, full), jnp.bfloat16),
            pltpu.VMEM((height, full), jnp.bfloat16),
            pltpu.VMEM((height, full), jnp.float32),
        ],
        compiler_params=pltpu.CompilerParams(vmem_limit_bytes=26 * 1024 * 1024),
        cost_estimate=pl.CostEstimate(flops=8 * 1024 * 1024 * height, bytes_accessed=24 * height * full, transcendentals=0),
    )(geo, polar_rows, cutoffs, got, tend, south, north, *tables)


def per_device(u_wind, v_wind, thickness, theta, polar_rows, cutoffs):
    levels, rows, cols = u_wind.shape
    lat_count = lax.axis_size("lat")
    count = lax.axis_size("lon")
    total_rows = rows * lat_count
    total_cols = cols * count
    dlon = 2.0 * math.pi / total_cols
    dlat = math.pi / total_rows
    step_size = 0.25 * dlon
    fields = (u_wind, v_wind, thickness, theta)
    per = levels // count

    got = lax.all_to_all(pack(count, fields), "lon", 0, 0, tiled=True)

    split_rows = got.reshape(count, per, 4, rows, cols)
    south = lax.ppermute(split_rows[:, :, :, rows - 1], "lat", [(i, i + 1) for i in range(lat_count - 1)])
    north = lax.ppermute(split_rows[:, :, :, 0], "lat", [(i + 1, i) for i in range(lat_count - 1)])

    geo = jnp.asarray(geometry(total_rows))
    cutoffs = cutoffs.reshape(total_rows // LANES, LANES)
    tables = fourier_tables(total_cols)
    tend = inner_tendencies(rows, dlon, dlat, geo, got)
    fresh = stepped(rows, dlon, dlat, step_size, geo, polar_rows, cutoffs, got, tend, south, north, tables)
    return tuple(place(lax.all_to_all(fresh, "lon", 0, 0, tiled=True), u_wind.shape))


def solution(mesh):
    field = P(None, "lat", "lon")
    return jax.shard_map(
        per_device,
        mesh=mesh,
        in_specs=(field, field, field, field, P(), P()),
        out_specs=(field, field, field, field),
        check_vma=False,
    )
```

```python
import functools
import math

import jax
import jax.numpy as jnp
import numpy as np
from jax import lax
from jax.experimental import pallas as pl
from jax.experimental.pallas import tpu as pltpu
from jax.sharding import PartitionSpec as P

OMEGA = 30.0
SECTORS = 8
REAL_Q = 64
FULL_Q = 128
SHIFT_Q = 52
LANES = 128


def geometry(total_rows):
    row = np.arange(-1, total_rows + 1)
    dist = np.maximum(np.minimum(row, total_rows - 1 - row), 0)
    cos_row = np.sin(np.pi * (dist + 0.5) / total_rows)
    face = np.arange(total_rows + 1)
    cos_face = np.sin(np.pi * np.minimum(face, total_rows - face) / total_rows)
    spin = -2.0 * OMEGA * np.cos(np.pi * (np.arange(total_rows) + 0.5) / total_rows)
    table = np.zeros((total_rows, 8))
    table[:, 0] = cos_row[1:-1]
    table[:, 1] = cos_row[:-2]
    table[:, 2] = cos_row[2:]
    table[:, 3] = cos_face[:-1]
    table[:, 4] = cos_face[1:]
    table[:, 5] = spin
    table[:, 6] = 1.0 / cos_row[1:-1]
    return table.astype(np.float32)


def split(x):
    high = x.astype(jnp.bfloat16)
    return high, (x - high.astype(jnp.float32)).astype(jnp.bfloat16)


def fourier_tables(total):
    column = np.arange(total // SECTORS)

    def angle(wave):
        return (column[:, None] * wave[None, :] % total) * (2.0 * np.pi / total)

    real, full = [], []
    for r in (0, 4):
        theta = angle(SECTORS * np.arange(REAL_Q) + r)
        real.append(np.concatenate([np.cos(theta), -np.sin(theta)], axis=1))
    for r in (1, 2, 3):
        theta = angle(SECTORS * (np.arange(FULL_Q) - SHIFT_Q) + r)
        cos, sin = np.cos(theta), np.sin(theta)
        full.append(np.block([[cos, -sin], [sin, cos]]))

    def halves(table):
        table = table.astype(np.float32)
        high = table.astype(jnp.bfloat16)
        return np.stack([high, (table - high.astype(np.float32)).astype(jnp.bfloat16)], axis=1)

    real, full = np.stack(real), np.stack(full)
    tables = (real, full, real.transpose(0, 2, 1), full.transpose(0, 2, 1))
    return [jnp.asarray(halves(t)) for t in tables]


def copy_all(pairs, sems):
    copies = [pltpu.make_async_copy(src, dst, sems.at[i]) for i, (src, dst) in enumerate(pairs)]
    for copy in copies:
        copy.start()
    for copy in copies:
        copy.wait()


def pack_body(count, per, rows, *refs):
    fields, out, sems = refs[:4], refs[4], refs[5]
    pairs = []
    for d in range(count):
        for k in range(per):
            for f in range(4):
                pairs.append((fields[f].at[d * per + k], out.at[d, pl.ds((4 * k + f) * rows, rows), :]))
    copy_all(pairs, sems)


def pack(count, fields):
    levels, rows, cols = fields[0].shape
    shape = (count, 4 * (levels // count) * rows, cols)
    return pl.pallas_call(
        functools.partial(pack_body, count, levels // count, rows),
        in_specs=[pl.BlockSpec(memory_space=pl.ANY)] * 4,
        out_specs=pl.BlockSpec(memory_space=pltpu.VMEM),
        out_shape=pltpu.VMEM(shape, jnp.float32),
        scratch_shapes=[pltpu.SemaphoreType.DMA((4 * levels,))],
        compiler_params=pltpu.CompilerParams(vmem_limit_bytes=8 * 1024 * 1024),
        cost_estimate=pl.CostEstimate(flops=0, bytes_accessed=8 * math.prod(shape), transcendentals=0),
    )(*[pltpu.with_memory_space_constraint(f, pltpu.HBM) for f in fields])


def place_body(count, per, rows, *refs):
    got, outs, sems = refs[0], refs[1:5], refs[5]
    pairs = []
    for d in range(count):
        for k in range(per):
            for f in range(4):
                pairs.append((got.at[d, pl.ds((4 * k + f) * rows, rows), :], outs[f].at[d * per + k]))
    copy_all(pairs, sems)


def place(got, shape):
    count = got.shape[0]
    return pl.pallas_call(
        functools.partial(place_body, count, shape[0] // count, shape[1]),
        in_specs=[pl.BlockSpec(memory_space=pltpu.VMEM)],
        out_specs=[pl.BlockSpec(memory_space=pl.ANY)] * 4,
        out_shape=[jax.ShapeDtypeStruct(shape, jnp.float32)] * 4,
        scratch_shapes=[pltpu.SemaphoreType.DMA((4 * shape[0],))],
        compiler_params=pltpu.CompilerParams(vmem_limit_bytes=32 * 1024 * 1024),
        cost_estimate=pl.CostEstimate(flops=0, bytes_accessed=8 * got.size, transcendentals=0),
    )(got)


def lat_shift(x, amount, edge):
    size = x.shape[0]
    place = lax.broadcasted_iota(jnp.int32, x.shape, 0)
    at = size - 1 if amount < 0 else 0
    return jnp.where(place == at, edge, pltpu.roll(x, amount % size, 0))


def group_tendencies(level, first, size, span, rows, cols, dlon, dlat, place, geo_ref, got_ref, halo_refs, tend_ref, skip=0):
    start = pl.multiple_of(level * 4 * rows, 4 * rows)
    geo = geo_ref[pl.ds(pl.multiple_of(place * rows + first, 8), size), :]
    fs, fn, spin0, inv = geo[0:1, 3:4], geo[:, 4:5], geo[:, 5:6], geo[:, 6:7]
    to_east = (0.5 / dlon) * inv
    to_south, to_north = (0.5 / dlat) * (geo[:, 1:2] * inv), (0.5 / dlat) * (geo[:, 2:3] * inv)
    out_x, out_y = (-1.0 / dlon) * inv, (-1.0 / dlat) * inv
    wide = span * cols + 2 * LANES
    signs = (-1.0, -1.0, 1.0, 1.0)

    def mid(x):
        return x[:, LANES : LANES + span * cols]

    def east_of(x):
        return pltpu.roll(x, wide - 1, 1)

    def west_of(x):
        return pltpu.roll(x, 1, 1)

    def joined(parts):
        return parts[0] if len(parts) == 1 else jnp.concatenate(parts, axis=1)

    def edge_row(f, r, row, side, at_pole):
        if 0 <= row < rows:
            return got_ref[r, pl.ds(start + f * rows + row, 1), :]
        near = 0 if row < 0 else rows - 1
        across = got_ref[(r + SECTORS // 2) % SECTORS, pl.ds(start + f * rows + near, 1), :]
        per = got_ref.shape[1] // (4 * rows)
        halo = halo_refs[side][pl.ds((r * per + level) * 4 + f, 1), :]
        return jnp.where(at_pole, signs[f] * across, halo)

    for base in range(0, SECTORS, span):
        sectors = range(base, base + span)
        ext, south, north = [], [], []
        for f in range(4):
            part = pl.ds(pl.multiple_of(start + f * rows + first, 8), size)
            ext.append(
                jnp.concatenate(
                    [got_ref[(base - 1) % SECTORS, part, cols - LANES :]]
                    + [got_ref[r, part, :] for r in sectors]
                    + [got_ref[(base + span) % SECTORS, part, :LANES]],
                    axis=1,
                )
            )
            south.append(joined([edge_row(f, r, first - 1, 0, place == 0) for r in sectors]))
            north.append(joined([edge_row(f, r, first + size, 1, place == lax.axis_size("lat") - 1) for r in sectors]))
        ux, vx, px, hx = ext
        heat_x = px * hx
        energy_x = 0.5 * (ux * ux + vx * vx) + heat_x
        u, v, p, heat, energy = mid(ux), mid(vx), mid(px), mid(heat_x), mid(energy_x)

        spin = spin0 + (mid(east_of(vx)) - mid(west_of(vx))) * to_east
        spin -= to_north * lat_shift(u, -1, north[0]) - to_south * lat_shift(u, 1, south[0])
        edges = [0.5 * (q[0] * q[0] + q[1] * q[1]) + q[2] * q[3] for q in (south, north)]
        de_x = mid(east_of(energy_x)) - mid(west_of(energy_x))
        de_y = lat_shift(energy, -1, edges[1]) - lat_shift(energy, 1, edges[0])
        u_t = spin * v - de_x * to_east
        v_t = de_y * (-0.5 / dlat) - spin * u

        a = 0.5 * (ux + east_of(ux))
        ap, am = jnp.maximum(a, 0.0), jnp.minimum(a, 0.0)
        flow_x = ap * px + am * east_of(px)
        hot_x = ap * heat_x + am * east_of(heat_x)
        b = (0.5 * fn) * (v + lat_shift(v, -1, north[1]))
        bp, bm = jnp.maximum(b, 0.0), jnp.minimum(b, 0.0)
        flow_y = bp * p + bm * lat_shift(p, -1, north[2])
        hot_y = bp * heat + bm * lat_shift(heat, -1, north[2] * north[3])
        b0 = (0.5 * fs) * (south[1] + v[0:1, :])
        bp0, bm0 = jnp.maximum(b0, 0.0), jnp.minimum(b0, 0.0)
        flow_y0 = bp0 * south[2] + bm0 * p[0:1, :]
        hot_y0 = bp0 * (south[2] * south[3]) + bm0 * heat[0:1, :]
        p_t = (mid(flow_x) - mid(west_of(flow_x))) * out_x + (flow_y - lat_shift(flow_y, 1, flow_y0)) * out_y
        h_t = (mid(hot_x) - mid(west_of(hot_x))) * out_x + (hot_y - lat_shift(hot_y, 1, hot_y0)) * out_y
        for f, value in enumerate((u_t, v_t, p_t, h_t)):
            kept = rows - 2 * skip
            part = pl.ds(pl.multiple_of(level * 4 * kept + f * kept + first - skip, 8), size)
            for i, r in enumerate(sectors):
                tend_ref[r, part, :] = value[:, i * cols : (i + 1) * cols]


def butterfly(rows_at, cols, tend_ref, high_ref, low_ref):
    x = [tend_ref[b, rows_at, :] for b in range(SECTORS)]
    s = [x[b] + x[b + 4] for b in range(4)]
    d = [x[b] - x[b + 4] for b in range(4)]
    c = math.sqrt(0.5)
    even, odd = s[0] + s[2], s[1] + s[3]
    plus, minus = c * (d[1] + d[3]), c * (d[1] - d[3])
    parts = (even + odd, even - odd, d[0] + minus, -d[2] - plus, s[0] - s[2], s[3] - s[1], d[0] - minus, d[2] - plus)
    for i, part in enumerate(parts):
        at = slice(i * cols, (i + 1) * cols)
        high_ref[rows_at, at], low_ref[rows_at, at] = split(part)


def product(high, low, table_ref, *index):
    big, small = table_ref[(*index, 0)], table_ref[(*index, 1)]
    total = jnp.dot(high, big, preferred_element_type=jnp.float32)
    total += jnp.dot(low, big, preferred_element_type=jnp.float32)
    return total + jnp.dot(high, small, preferred_element_type=jnp.float32)


def truncate(total, cols, limit, tables, high_ref, low_ref, wave_ref):
    real_ref, full_ref, real_back_ref, full_back_ref = tables
    for i, r in enumerate((0, 4, 1, 2, 3)):
        if i < 2:
            at, half = slice(i * cols, (i + 1) * cols), REAL_Q
            ahead, back, place = real_ref, real_back_ref, i
        else:
            at, half = slice((2 * i - 2) * cols, 2 * i * cols), FULL_Q
            ahead, back, place = full_ref, full_back_ref, i - 2
        spectrum = product(high_ref[:, at], low_ref[:, at], ahead, place)
        lane = lax.broadcasted_iota(jnp.int32, (1, 2 * half), 1)
        q = jnp.where(lane >= half, lane - half, lane) - (0 if i < 2 else SHIFT_Q)
        k = jnp.abs(SECTORS * q + r)
        factor = jnp.where(k <= limit, jnp.where(k == 0, 1.0 / total, 2.0 / total), 0.0)
        wave_ref[:, at] = product(*split(spectrum * factor), back, place)


def update(level, rows, cols, step_size, listed, got_ref, tend_ref, wave_ref, out_ref):
    c = math.sqrt(0.5)
    high = 4 * rows
    for f in range(4):
        for j in range(0, rows, 8):
            at = pl.ds(pl.multiple_of(level * high + f * rows + j, 8), 8)
            w0, w4, a1, b1, a2, b2, a3, b3 = [wave_ref[at, i * cols : (i + 1) * cols] for i in range(SECTORS)]
            near, far = w0 + w4, w0 - w4
            even = (near + a2, far - b2, near - a2, far + b2)
            odd = (a1 + a3, c * ((a1 - b1) - (a3 + b3)), b3 - b1, c * ((a3 - b3) - (a1 + b1)))
            chosen = listed[j : j + 8, :]
            for b in range(SECTORS):
                smooth = even[b % 4] + odd[b % 4] if b < 4 else even[b % 4] - odd[b % 4]
                base = got_ref[b, at, :]
                if f == 3:
                    base = base * got_ref[b, pl.ds(pl.multiple_of(level * high + 2 * rows + j, 8), 8), :]
                out_ref[b, at, :] = base + step_size * jnp.where(chosen, smooth, tend_ref[b, at, :])


def edges_body(per, rows, got_ref, low_ref, high_ref, held_ref, sems):
    parts = range(4 * per)
    pairs = [(got_ref.at[:, pl.ds(q * rows, 8), :], held_ref.at[0, q]) for q in parts]
    pairs += [(got_ref.at[:, pl.ds((q + 1) * rows - 8, 8), :], held_ref.at[1, q]) for q in parts]
    copy_all(pairs, sems)
    for r in range(SECTORS):
        for q in parts:
            at = r * 4 * per + q
            low_ref[at : at + 1, :] = held_ref[0, q, r, 0:1, :]
            high_ref[at : at + 1, :] = held_ref[1, q, r, 7:8, :]


def edge_rows(rows, got):
    count, height, cols = got.shape
    inside = pl.BlockSpec(memory_space=pltpu.VMEM)
    return pl.pallas_call(
        functools.partial(edges_body, height // (4 * rows), rows),
        in_specs=[pl.BlockSpec(memory_space=pltpu.HBM)],
        out_specs=[inside] * 2,
        out_shape=[jax.ShapeDtypeStruct((count * height // rows, cols), jnp.float32)] * 2,
        scratch_shapes=[
            pltpu.VMEM((2, height // rows, count, 8, cols), jnp.float32),
            pltpu.SemaphoreType.DMA((2 * height // rows,)),
        ],
        compiler_params=pltpu.CompilerParams(vmem_limit_bytes=8 * 1024 * 1024),
        cost_estimate=pl.CostEstimate(flops=0, bytes_accessed=16 * count * height // rows * cols, transcendentals=0),
    )(got)


def arrivals(per, high, far_ref, near_ref, sems):
    def one(level):
        at = pl.ds(pl.multiple_of(level * high, high), high)
        return pltpu.make_async_copy(far_ref.at[:, at, :], near_ref.at[:, at, :], sems.at[level])

    for level in range(per):
        one(level).start()
    return one


def inner_body(per, rows, cols, dlon, dlat, geo_ref, far_ref, tend_ref, got_ref, sems):
    place = lax.axis_index("lat")
    arrival = arrivals(per, 4 * rows, far_ref, got_ref, sems)

    @pl.loop(0, per)
    def _(level):
        arrival(level).wait()
        for first in range(8, rows - 8, 8):
            group_tendencies(level, first, 8, 2, rows, cols, dlon, dlat, place, geo_ref, got_ref, None, tend_ref, 8)


def inner_tendencies(rows, dlon, dlat, geo, got):
    inside = pl.BlockSpec(memory_space=pltpu.VMEM)
    return pl.pallas_call(
        functools.partial(inner_body, got.shape[1] // (4 * rows), rows, got.shape[2], dlon, dlat),
        in_specs=[inside, pl.BlockSpec(memory_space=pltpu.HBM)],
        out_specs=inside,
        scratch_shapes=[pltpu.VMEM(got.shape, jnp.float32), pltpu.SemaphoreType.DMA((got.shape[1] // (4 * rows),))],
        out_shape=jax.ShapeDtypeStruct((got.shape[0], got.shape[1] // rows * (rows - 16), got.shape[2]), jnp.float32),
        compiler_params=pltpu.CompilerParams(vmem_limit_bytes=12 * 1024 * 1024),
        cost_estimate=pl.CostEstimate(flops=40 * got.size, bytes_accessed=6 * got.size, transcendentals=0),
    )(geo, got)


def step_body(per, rows, cols, dlon, dlat, step_size, geo_ref, polar_ref, cutoff_ref, far_ref, tend_ref, south_ref, north_ref, *refs):
    tables = refs[:4]
    out_ref, edge_ref, high_ref, low_ref, wave_ref, got_ref, sems = refs[4:]
    high = 4 * rows
    arrival = arrivals(per, high, far_ref, got_ref, sems)
    halos = (south_ref, north_ref)
    place = lax.axis_index("lat")
    total = rows * lax.axis_size("lat")
    edge = jnp.sum((polar_ref[...] < total // 2).astype(jnp.int32))
    own = place * rows + lax.broadcasted_iota(jnp.int32, (rows, 1), 0)
    listed = (own < edge) | (own >= total // 2 + edge)
    bands = LANES // rows
    cut = cutoff_ref[pl.ds(place // bands, 1), :]
    lane = lax.broadcasted_iota(jnp.int32, (rows, LANES), 1)
    mine = lane == lax.rem(place, bands) * rows + lax.broadcasted_iota(jnp.int32, (rows, LANES), 0)
    limit = jnp.sum(jnp.where(mine, cut, 0), axis=1, keepdims=True)
    limit = jnp.concatenate([limit] * (4 * per), axis=0)

    @pl.loop(0, per)
    def _(level):
        arrival(level).wait()
        for first in (0, rows - 8):
            group_tendencies(level, first, 8, 2, rows, cols, dlon, dlat, place, geo_ref, got_ref, halos, edge_ref)
        for f in range(4):
            part = pl.ds(pl.multiple_of(level * high + f * rows + 8, 8), rows - 16)
            kept = pl.ds(pl.multiple_of((level * 4 + f) * (rows - 16), 8), rows - 16)
            for r in range(SECTORS):
                edge_ref[r, part, :] = tend_ref[r, kept, :]

    @pl.loop(0, per * high // 16)
    def _(group):
        butterfly(pl.ds(pl.multiple_of(group * 16, 16), 16), cols, edge_ref, high_ref, low_ref)

    truncate(SECTORS * cols, cols, limit, tables, high_ref, low_ref, wave_ref)

    @pl.loop(0, per)
    def _(level):
        update(level, rows, cols, step_size, listed, got_ref, edge_ref, wave_ref, out_ref)


def stepped(rows, dlon, dlat, step_size, geo, polar_rows, cutoffs, got, tend, south, north, tables):
    count, height, cols = got.shape
    inside = pl.BlockSpec(memory_space=pltpu.VMEM)
    full = count * cols
    return pl.pallas_call(
        functools.partial(step_body, height // (4 * rows), rows, cols, dlon, dlat, step_size),
        in_specs=[inside] * 3 + [pl.BlockSpec(memory_space=pltpu.HBM)] + [inside] * 7,
        out_specs=inside,
        out_shape=jax.ShapeDtypeStruct(got.shape, jnp.float32),
        scratch_shapes=[
            pltpu.VMEM(got.shape, jnp.float32),
            pltpu.VMEM((height, full), jnp.bfloat16),
            pltpu.VMEM((height, full), jnp.bfloat16),
            pltpu.VMEM((height, full), jnp.float32),
            pltpu.VMEM(got.shape, jnp.float32),
            pltpu.SemaphoreType.DMA((height // (4 * rows),)),
        ],
        compiler_params=pltpu.CompilerParams(vmem_limit_bytes=32 * 1024 * 1024),
        cost_estimate=pl.CostEstimate(flops=8 * 1024 * 1024 * height, bytes_accessed=24 * height * full, transcendentals=0),
    )(geo, polar_rows, cutoffs, got, tend, south, north, *tables)


def per_device(u_wind, v_wind, thickness, theta, polar_rows, cutoffs):
    levels, rows, cols = u_wind.shape
    lat_count = lax.axis_size("lat")
    count = lax.axis_size("lon")
    total_rows = rows * lat_count
    total_cols = cols * count
    dlon = 2.0 * math.pi / total_cols
    dlat = math.pi / total_rows
    step_size = 0.25 * dlon
    fields = (u_wind, v_wind, thickness, theta)
    per = levels // count

    got = lax.all_to_all(pack(count, fields), "lon", 0, 0, tiled=True)

    got = pltpu.with_memory_space_constraint(got, pltpu.HBM)
    low_rows, high_rows = edge_rows(rows, got)
    south = lax.ppermute(high_rows, "lat", [(i, i + 1) for i in range(lat_count - 1)])
    north = lax.ppermute(low_rows, "lat", [(i + 1, i) for i in range(lat_count - 1)])

    geo = jnp.asarray(geometry(total_rows))
    cutoffs = cutoffs.reshape(total_rows // LANES, LANES)
    tables = fourier_tables(total_cols)
    tend = inner_tendencies(rows, dlon, dlat, geo, got)
    fresh = stepped(rows, dlon, dlat, step_size, geo, polar_rows, cutoffs, got, tend, south, north, tables)
    return tuple(place(lax.all_to_all(fresh, "lon", 0, 0, tiled=True), u_wind.shape))


def solution(mesh):
    field = P(None, "lat", "lon")
    return jax.shard_map(
        per_device,
        mesh=mesh,
        in_specs=(field, field, field, field, P(), P()),
        out_specs=(field, field, field, field),
        check_vma=False,
    )
```

```python
import functools
import math

import jax
import jax.numpy as jnp
import numpy as np
from jax import lax
from jax.experimental import pallas as pl
from jax.experimental.pallas import tpu as pltpu
from jax.sharding import PartitionSpec as P

OMEGA = 30.0
SECTORS = 8
REAL_Q = 64
FULL_Q = 128
SHIFT_Q = 52
LANES = 128


def geometry(total_rows):
    row = np.arange(-1, total_rows + 1)
    dist = np.maximum(np.minimum(row, total_rows - 1 - row), 0)
    cos_row = np.sin(np.pi * (dist + 0.5) / total_rows)
    face = np.arange(total_rows + 1)
    cos_face = np.sin(np.pi * np.minimum(face, total_rows - face) / total_rows)
    spin = -2.0 * OMEGA * np.cos(np.pi * (np.arange(total_rows) + 0.5) / total_rows)
    table = np.zeros((total_rows, 8))
    table[:, 0] = cos_row[1:-1]
    table[:, 1] = cos_row[:-2]
    table[:, 2] = cos_row[2:]
    table[:, 3] = cos_face[:-1]
    table[:, 4] = cos_face[1:]
    table[:, 5] = spin
    table[:, 6] = 1.0 / cos_row[1:-1]
    return table.astype(np.float32)


def split(x):
    high = x.astype(jnp.bfloat16)
    return high, (x - high.astype(jnp.float32)).astype(jnp.bfloat16)


def fourier_tables(total):
    cols = total // SECTORS
    column = np.arange(cols)

    def angle(wave):
        return (column[:, None] * wave[None, :] % total) * (2.0 * np.pi / total)

    real = []
    for r in (0, 4):
        theta = angle(SECTORS * np.arange(REAL_Q) + r)
        real.append(np.concatenate([np.cos(theta), -np.sin(theta)], axis=1))
    gap = np.zeros_like(real[0])
    tables = [np.block([[real[0], gap], [gap, real[1]]])]
    for r in (1, 2, 3):
        theta = angle(SECTORS * (np.arange(FULL_Q) - SHIFT_Q) + r)
        cos, sin = np.cos(theta), np.sin(theta)
        tables.append(np.block([[cos, -sin], [sin, cos]]))

    def halves(table):
        table = table.astype(np.float32)
        high = table.astype(jnp.bfloat16)
        return np.stack([high, (table - high.astype(np.float32)).astype(jnp.bfloat16)], axis=1)

    tables = np.stack(tables)
    return [jnp.asarray(halves(t)) for t in (tables, tables.transpose(0, 2, 1))]


def copy_all(pairs, sems):
    copies = [pltpu.make_async_copy(src, dst, sems.at[i]) for i, (src, dst) in enumerate(pairs)]
    for copy in copies:
        copy.start()
    for copy in copies:
        copy.wait()


def pack_body(count, per, rows, *refs):
    fields, out, sems = refs[:4], refs[4], refs[5]
    pairs = []
    for d in range(count):
        for k in range(per):
            for f in range(4):
                pairs.append((fields[f].at[d * per + k], out.at[d, pl.ds((4 * k + f) * rows, rows), :]))
    copy_all(pairs, sems)


def pack(count, fields):
    levels, rows, cols = fields[0].shape
    shape = (count, 4 * (levels // count) * rows, cols)
    return pl.pallas_call(
        functools.partial(pack_body, count, levels // count, rows),
        in_specs=[pl.BlockSpec(memory_space=pl.ANY)] * 4,
        out_specs=pl.BlockSpec(memory_space=pltpu.VMEM),
        out_shape=pltpu.VMEM(shape, jnp.float32),
        scratch_shapes=[pltpu.SemaphoreType.DMA((4 * levels,))],
        compiler_params=pltpu.CompilerParams(vmem_limit_bytes=8 * 1024 * 1024),
        cost_estimate=pl.CostEstimate(flops=0, bytes_accessed=8 * math.prod(shape), transcendentals=0),
    )(*[pltpu.with_memory_space_constraint(f, pltpu.HBM) for f in fields])


def place_body(count, per, rows, *refs):
    got, outs, sems = refs[0], refs[1:5], refs[5]
    pairs = []
    for d in range(count):
        for k in range(per):
            for f in range(4):
                pairs.append((got.at[d, pl.ds((4 * k + f) * rows, rows), :], outs[f].at[d * per + k]))
    copy_all(pairs, sems)


def place(got, shape):
    count = got.shape[0]
    return pl.pallas_call(
        functools.partial(place_body, count, shape[0] // count, shape[1]),
        in_specs=[pl.BlockSpec(memory_space=pltpu.VMEM)],
        out_specs=[pl.BlockSpec(memory_space=pl.ANY)] * 4,
        out_shape=[jax.ShapeDtypeStruct(shape, jnp.float32)] * 4,
        scratch_shapes=[pltpu.SemaphoreType.DMA((4 * shape[0],))],
        compiler_params=pltpu.CompilerParams(vmem_limit_bytes=32 * 1024 * 1024),
        cost_estimate=pl.CostEstimate(flops=0, bytes_accessed=8 * got.size, transcendentals=0),
    )(got)


def lat_shift(x, amount, edge):
    size = x.shape[0]
    place = lax.broadcasted_iota(jnp.int32, x.shape, 0)
    at = size - 1 if amount < 0 else 0
    return jnp.where(place == at, edge, pltpu.roll(x, amount % size, 0))


def group_tendencies(level, first, size, span, rows, cols, dlon, dlat, place, geo_ref, got_ref, halo_refs, tend_ref, skip=0):
    start = pl.multiple_of(level * 4 * rows, 4 * rows)
    geo = geo_ref[pl.ds(pl.multiple_of(place * rows + first, 8), size), :]
    fs, fn, spin0, inv = geo[0:1, 3:4], geo[:, 4:5], geo[:, 5:6], geo[:, 6:7]
    to_east = (0.5 / dlon) * inv
    to_south, to_north = (0.5 / dlat) * (geo[:, 1:2] * inv), (0.5 / dlat) * (geo[:, 2:3] * inv)
    out_x, out_y = (-1.0 / dlon) * inv, (-1.0 / dlat) * inv
    wide = span * cols + 2 * LANES
    signs = (-1.0, -1.0, 1.0, 1.0)

    def mid(x):
        return x[:, LANES : LANES + span * cols]

    def east_of(x):
        return pltpu.roll(x, wide - 1, 1)

    def west_of(x):
        return pltpu.roll(x, 1, 1)

    def joined(parts):
        return parts[0] if len(parts) == 1 else jnp.concatenate(parts, axis=1)

    def edge_row(f, r, row, side, at_pole):
        if 0 <= row < rows:
            return got_ref[r, pl.ds(start + f * rows + row, 1), :]
        near = 0 if row < 0 else rows - 1
        across = got_ref[(r + SECTORS // 2) % SECTORS, pl.ds(start + f * rows + near, 1), :]
        per = got_ref.shape[1] // (4 * rows)
        at = pl.ds((r * per + level) * 4 + f, 1)
        halo = jnp.where(lax.rem(place, 2) == 1, halo_refs[side][at, :], halo_refs[1 - side][at, :])
        return jnp.where(at_pole, signs[f] * across, halo)

    for base in range(0, SECTORS, span):
        sectors = range(base, base + span)
        ext, south, north = [], [], []
        for f in range(4):
            part = pl.ds(pl.multiple_of(start + f * rows + first, 8), size)
            ext.append(
                jnp.concatenate(
                    [got_ref[(base - 1) % SECTORS, part, cols - LANES :]]
                    + [got_ref[r, part, :] for r in sectors]
                    + [got_ref[(base + span) % SECTORS, part, :LANES]],
                    axis=1,
                )
            )
            south.append(joined([edge_row(f, r, first - 1, 0, place == 0) for r in sectors]))
            north.append(joined([edge_row(f, r, first + size, 1, place == lax.axis_size("lat") - 1) for r in sectors]))
        ux, vx, px, hx = ext
        heat_x = px * hx
        energy_x = 0.5 * (ux * ux + vx * vx) + heat_x
        u, v, p, heat, energy = mid(ux), mid(vx), mid(px), mid(heat_x), mid(energy_x)

        spin = spin0 + (mid(east_of(vx)) - mid(west_of(vx))) * to_east
        spin -= to_north * lat_shift(u, -1, north[0]) - to_south * lat_shift(u, 1, south[0])
        edges = [0.5 * (q[0] * q[0] + q[1] * q[1]) + q[2] * q[3] for q in (south, north)]
        de_x = mid(east_of(energy_x)) - mid(west_of(energy_x))
        de_y = lat_shift(energy, -1, edges[1]) - lat_shift(energy, 1, edges[0])
        u_t = spin * v - de_x * to_east
        v_t = de_y * (-0.5 / dlat) - spin * u

        a = 0.5 * (ux + east_of(ux))
        ap, am = jnp.maximum(a, 0.0), jnp.minimum(a, 0.0)
        flow_x = ap * px + am * east_of(px)
        hot_x = ap * heat_x + am * east_of(heat_x)
        b = (0.5 * fn) * (v + lat_shift(v, -1, north[1]))
        bp, bm = jnp.maximum(b, 0.0), jnp.minimum(b, 0.0)
        flow_y = bp * p + bm * lat_shift(p, -1, north[2])
        hot_y = bp * heat + bm * lat_shift(heat, -1, north[2] * north[3])
        b0 = (0.5 * fs) * (south[1] + v[0:1, :])
        bp0, bm0 = jnp.maximum(b0, 0.0), jnp.minimum(b0, 0.0)
        flow_y0 = bp0 * south[2] + bm0 * p[0:1, :]
        hot_y0 = bp0 * (south[2] * south[3]) + bm0 * heat[0:1, :]
        p_t = (mid(flow_x) - mid(west_of(flow_x))) * out_x + (flow_y - lat_shift(flow_y, 1, flow_y0)) * out_y
        h_t = (mid(hot_x) - mid(west_of(hot_x))) * out_x + (hot_y - lat_shift(hot_y, 1, hot_y0)) * out_y
        for f, value in enumerate((u_t, v_t, p_t, h_t)):
            kept = rows - 2 * skip
            part = pl.ds(pl.multiple_of(level * 4 * kept + f * kept + first - skip, 8), size)
            for i, r in enumerate(sectors):
                tend_ref[r, part, :] = value[:, i * cols : (i + 1) * cols]


def butterfly(group, cols, tend_ref, parts_ref):
    half = parts_ref.shape[0] // 2
    rows_at = pl.ds(pl.multiple_of(group * 16, 16), 16)
    low_at = pl.ds(pl.multiple_of(half + group * 16, 16), 16)
    x = [tend_ref[b, rows_at, :] for b in range(SECTORS)]
    s = [x[b] + x[b + 4] for b in range(4)]
    d = [x[b] - x[b + 4] for b in range(4)]
    c = math.sqrt(0.5)
    even, odd = s[0] + s[2], s[1] + s[3]
    plus, minus = c * (d[1] + d[3]), c * (d[1] - d[3])
    parts = (even + odd, even - odd, d[0] + minus, -d[2] - plus, s[0] - s[2], s[3] - s[1], d[0] - minus, d[2] - plus)
    for i, part in enumerate(parts):
        at = slice(i * cols, (i + 1) * cols)
        parts_ref[rows_at, at], parts_ref[low_at, at] = split(part)


def product(parts, table_ref, place):
    half = parts.shape[0] // 2
    total = jnp.dot(parts, table_ref[place, 0], preferred_element_type=jnp.float32)
    small = jnp.dot(parts[:half], table_ref[place, 1], preferred_element_type=jnp.float32)
    return total[:half] + (total[half:] + small)


def truncate(total, cols, limit, ahead_ref, back_ref, parts_ref, wave_ref):
    lane = lax.broadcasted_iota(jnp.int32, (1, 2 * FULL_Q), 1)
    for r in range(4):
        at = slice(2 * r * cols, (2 * r + 2) * cols)
        spectrum = product(parts_ref[:, at], ahead_ref, r)
        if r == 0:
            k = SECTORS * lax.rem(lane, REAL_Q) + jnp.where(lane >= FULL_Q, 4, 0)
        else:
            k = jnp.abs(SECTORS * (lax.rem(lane, FULL_Q) - SHIFT_Q) + r)
        factor = jnp.where(k <= limit, jnp.where(k == 0, 1.0 / total, 2.0 / total), 0.0)
        wave_ref[:, at] = product(jnp.concatenate(split(spectrum * factor), axis=0), back_ref, r)


def update(level, rows, cols, step_size, listed, got_ref, tend_ref, wave_ref, out_ref):
    c = math.sqrt(0.5)
    high = 4 * rows
    for f in range(4):
        for j in range(0, rows, 8):
            at = pl.ds(pl.multiple_of(level * high + f * rows + j, 8), 8)
            w0, w4, a1, b1, a2, b2, a3, b3 = [wave_ref[at, i * cols : (i + 1) * cols] for i in range(SECTORS)]
            near, far = w0 + w4, w0 - w4
            even = (near + a2, far - b2, near - a2, far + b2)
            odd = (a1 + a3, c * ((a1 - b1) - (a3 + b3)), b3 - b1, c * ((a3 - b3) - (a1 + b1)))
            chosen = listed[j : j + 8, :]
            for b in range(SECTORS):
                smooth = even[b % 4] + odd[b % 4] if b < 4 else even[b % 4] - odd[b % 4]
                base = got_ref[b, at, :]
                if f == 3:
                    base = base * got_ref[b, pl.ds(pl.multiple_of(level * high + 2 * rows + j, 8), 8), :]
                out_ref[b, at, :] = base + step_size * jnp.where(chosen, smooth, tend_ref[b, at, :])


def edges_body(per, rows, got_ref, inner_ref, outer_ref, held_ref, sems):
    parts = range(4 * per)
    pairs = [(got_ref.at[:, pl.ds(q * rows, 8), :], held_ref.at[0, q]) for q in parts]
    pairs += [(got_ref.at[:, pl.ds((q + 1) * rows - 8, 8), :], held_ref.at[1, q]) for q in parts]
    copy_all(pairs, sems)
    odd = lax.rem(lax.axis_index("lat"), 2) == 1
    for r in range(SECTORS):
        for q in parts:
            at = r * 4 * per + q
            low, high = held_ref[0, q, r, 0:1, :], held_ref[1, q, r, 7:8, :]
            inner_ref[at : at + 1, :] = jnp.where(odd, low, high)
            outer_ref[at : at + 1, :] = jnp.where(odd, high, low)


def edge_rows(rows, got):
    count, height, cols = got.shape
    inside = pl.BlockSpec(memory_space=pltpu.VMEM)
    return pl.pallas_call(
        functools.partial(edges_body, height // (4 * rows), rows),
        in_specs=[pl.BlockSpec(memory_space=pltpu.HBM)],
        out_specs=[inside] * 2,
        out_shape=[jax.ShapeDtypeStruct((count * height // rows, cols), jnp.float32)] * 2,
        scratch_shapes=[
            pltpu.VMEM((2, height // rows, count, 8, cols), jnp.float32),
            pltpu.SemaphoreType.DMA((2 * height // rows,)),
        ],
        compiler_params=pltpu.CompilerParams(vmem_limit_bytes=8 * 1024 * 1024),
        cost_estimate=pl.CostEstimate(flops=0, bytes_accessed=16 * count * height // rows * cols, transcendentals=0),
    )(got)


def arrivals(per, high, far_ref, near_ref, sems):
    def one(level):
        at = pl.ds(pl.multiple_of(level * high, high), high)
        return pltpu.make_async_copy(far_ref.at[:, at, :], near_ref.at[:, at, :], sems.at[level])

    for level in range(per):
        one(level).start()
    return one


def inner_body(per, rows, cols, dlon, dlat, geo_ref, far_ref, tend_ref, got_ref, sems):
    place = lax.axis_index("lat")
    arrival = arrivals(per, 4 * rows, far_ref, got_ref, sems)

    @pl.loop(0, per)
    def _(level):
        arrival(level).wait()
        for first in range(8, rows - 8, 8):
            group_tendencies(level, first, 8, 2, rows, cols, dlon, dlat, place, geo_ref, got_ref, None, tend_ref, 8)


def inner_tendencies(rows, dlon, dlat, geo, got):
    inside = pl.BlockSpec(memory_space=pltpu.VMEM)
    return pl.pallas_call(
        functools.partial(inner_body, got.shape[1] // (4 * rows), rows, got.shape[2], dlon, dlat),
        in_specs=[inside, pl.BlockSpec(memory_space=pltpu.HBM)],
        out_specs=inside,
        scratch_shapes=[pltpu.VMEM(got.shape, jnp.float32), pltpu.SemaphoreType.DMA((got.shape[1] // (4 * rows),))],
        out_shape=jax.ShapeDtypeStruct((got.shape[0], got.shape[1] // rows * (rows - 16), got.shape[2]), jnp.float32),
        compiler_params=pltpu.CompilerParams(vmem_limit_bytes=12 * 1024 * 1024),
        cost_estimate=pl.CostEstimate(flops=40 * got.size, bytes_accessed=6 * got.size, transcendentals=0),
    )(geo, got)


def step_body(per, rows, cols, dlon, dlat, step_size, geo_ref, polar_ref, cutoff_ref, far_ref, tend_ref, inner_ref, outer_ref, *refs):
    ahead_ref, back_ref, out_ref, edge_ref, parts_ref, wave_ref, got_ref, sems = refs
    high = 4 * rows
    arrival = arrivals(per, high, far_ref, got_ref, sems)
    halos = (inner_ref, outer_ref)
    place = lax.axis_index("lat")
    total = rows * lax.axis_size("lat")
    edge = jnp.sum((polar_ref[...] < total // 2).astype(jnp.int32))
    own = place * rows + lax.broadcasted_iota(jnp.int32, (rows, 1), 0)
    listed = (own < edge) | (own >= total // 2 + edge)
    bands = LANES // rows
    cut = cutoff_ref[pl.ds(place // bands, 1), :]
    lane = lax.broadcasted_iota(jnp.int32, (rows, LANES), 1)
    mine = lane == lax.rem(place, bands) * rows + lax.broadcasted_iota(jnp.int32, (rows, LANES), 0)
    limit = jnp.sum(jnp.where(mine, cut, 0), axis=1, keepdims=True)
    limit = jnp.concatenate([limit] * (4 * per), axis=0)

    @pl.loop(0, per)
    def _(level):
        arrival(level).wait()
        for first in (0, rows - 8):
            group_tendencies(level, first, 8, 2, rows, cols, dlon, dlat, place, geo_ref, got_ref, halos, edge_ref)
        for f in range(4):
            part = pl.ds(pl.multiple_of(level * high + f * rows + 8, 8), rows - 16)
            kept = pl.ds(pl.multiple_of((level * 4 + f) * (rows - 16), 8), rows - 16)
            for r in range(SECTORS):
                edge_ref[r, part, :] = tend_ref[r, kept, :]

    @pl.loop(0, per * high // 16)
    def _(group):
        butterfly(group, cols, edge_ref, parts_ref)

    truncate(SECTORS * cols, cols, limit, ahead_ref, back_ref, parts_ref, wave_ref)

    @pl.loop(0, per)
    def _(level):
        update(level, rows, cols, step_size, listed, got_ref, edge_ref, wave_ref, out_ref)


def stepped(rows, dlon, dlat, step_size, geo, polar_rows, cutoffs, got, tend, inner, outer, tables):
    count, height, cols = got.shape
    inside = pl.BlockSpec(memory_space=pltpu.VMEM)
    full = count * cols
    return pl.pallas_call(
        functools.partial(step_body, height // (4 * rows), rows, cols, dlon, dlat, step_size),
        in_specs=[inside] * 3 + [pl.BlockSpec(memory_space=pltpu.HBM)] + [inside] * 5,
        out_specs=inside,
        out_shape=jax.ShapeDtypeStruct(got.shape, jnp.float32),
        scratch_shapes=[
            pltpu.VMEM(got.shape, jnp.float32),
            pltpu.VMEM((2 * height, full), jnp.bfloat16),
            pltpu.VMEM((height, full), jnp.float32),
            pltpu.VMEM(got.shape, jnp.float32),
            pltpu.SemaphoreType.DMA((height // (4 * rows),)),
        ],
        compiler_params=pltpu.CompilerParams(vmem_limit_bytes=32 * 1024 * 1024),
        cost_estimate=pl.CostEstimate(flops=8 * 1024 * 1024 * height, bytes_accessed=24 * height * full, transcendentals=0),
    )(geo, polar_rows, cutoffs, got, tend, inner, outer, *tables)


def per_device(u_wind, v_wind, thickness, theta, polar_rows, cutoffs):
    levels, rows, cols = u_wind.shape
    lat_count = lax.axis_size("lat")
    count = lax.axis_size("lon")
    total_rows = rows * lat_count
    total_cols = cols * count
    dlon = 2.0 * math.pi / total_cols
    dlat = math.pi / total_rows
    step_size = 0.25 * dlon
    fields = (u_wind, v_wind, thickness, theta)
    per = levels // count

    got = lax.all_to_all(pack(count, fields), "lon", 0, 0, tiled=True)

    got = pltpu.with_memory_space_constraint(got, pltpu.HBM)
    inner, outer = edge_rows(rows, got)
    across = [(i, i + 1) for i in range(1, lat_count - 1, 2)]
    within = [(i, i + 1) for i in range(0, lat_count, 2)]
    outer = lax.ppermute(outer, "lat", across + [(j, i) for i, j in across])
    inner = lax.ppermute(inner, "lat", within + [(j, i) for i, j in within])

    geo = jnp.asarray(geometry(total_rows))
    cutoffs = cutoffs.reshape(total_rows // LANES, LANES)
    tables = fourier_tables(total_cols)
    tend = inner_tendencies(rows, dlon, dlat, geo, got)
    fresh = stepped(rows, dlon, dlat, step_size, geo, polar_rows.T, cutoffs, got, tend, inner, outer, tables)
    return tuple(place(lax.all_to_all(fresh, "lon", 0, 0, tiled=True), u_wind.shape))


def solution(mesh):
    field = P(None, "lat", "lon")
    return jax.shard_map(
        per_device,
        mesh=mesh,
        in_specs=(field, field, field, field, P(), P()),
        out_specs=(field, field, field, field),
        check_vma=False,
    )
```

```python
import functools
import math

import jax
import jax.numpy as jnp
import numpy as np
from jax import lax
from jax.experimental import pallas as pl
from jax.experimental.pallas import tpu as pltpu
from jax.sharding import PartitionSpec as P

OMEGA = 30.0
SECTORS = 8
REAL_Q = 64
FULL_Q = 128
SHIFT_Q = 52
LANES = 128


def geometry(total_rows):
    row = np.arange(-1, total_rows + 1)
    dist = np.maximum(np.minimum(row, total_rows - 1 - row), 0)
    cos_row = np.sin(np.pi * (dist + 0.5) / total_rows)
    face = np.arange(total_rows + 1)
    cos_face = np.sin(np.pi * np.minimum(face, total_rows - face) / total_rows)
    spin = -2.0 * OMEGA * np.cos(np.pi * (np.arange(total_rows) + 0.5) / total_rows)
    table = np.zeros((total_rows, 8))
    table[:, 0] = cos_row[1:-1]
    table[:, 1] = cos_row[:-2]
    table[:, 2] = cos_row[2:]
    table[:, 3] = cos_face[:-1]
    table[:, 4] = cos_face[1:]
    table[:, 5] = spin
    table[:, 6] = 1.0 / cos_row[1:-1]
    return table.astype(np.float32)


def split(x):
    high = x.astype(jnp.bfloat16)
    return high, (x - high.astype(jnp.float32)).astype(jnp.bfloat16)


def fourier_tables(total):
    cols = total // SECTORS
    column = np.arange(cols)

    def angle(wave):
        return (column[:, None] * wave[None, :] % total) * (2.0 * np.pi / total)

    real = []
    for r in (0, 4):
        theta = angle(SECTORS * np.arange(REAL_Q) + r)
        real.append(np.concatenate([np.cos(theta), -np.sin(theta)], axis=1))
    gap = np.zeros_like(real[0])
    tables = [np.block([[real[0], gap], [gap, real[1]]])]
    for r in (1, 2, 3):
        theta = angle(SECTORS * (np.arange(FULL_Q) - SHIFT_Q) + r)
        cos, sin = np.cos(theta), np.sin(theta)
        tables.append(np.block([[cos, -sin], [sin, cos]]))

    def halves(table):
        table = table.astype(np.float32)
        high = table.astype(jnp.bfloat16)
        return np.concatenate([high, high, (table - high.astype(np.float32)).astype(jnp.bfloat16)], axis=1)

    tables = np.stack(tables)
    return [jnp.asarray(halves(t)) for t in (tables, tables.transpose(0, 2, 1))]


def copy_all(pairs, sems):
    copies = [pltpu.make_async_copy(src, dst, sems.at[i]) for i, (src, dst) in enumerate(pairs)]
    for copy in copies:
        copy.start()
    for copy in copies:
        copy.wait()


def pack_body(count, per, *refs):
    fields, out, sems = refs[:4], refs[4], refs[5]
    copy_all([(fields[f].at[pl.ds(d * per, per)], out.at[d, :, f]) for d in range(count) for f in range(4)], sems)


def pack(count, fields):
    levels, rows, cols = fields[0].shape
    shape = (count, levels // count, 4, rows, cols)
    packed = pl.pallas_call(
        functools.partial(pack_body, count, levels // count),
        in_specs=[pl.BlockSpec(memory_space=pl.ANY)] * 4,
        out_specs=pl.BlockSpec(memory_space=pltpu.VMEM),
        out_shape=pltpu.VMEM(shape, jnp.float32),
        scratch_shapes=[pltpu.SemaphoreType.DMA((4 * count,))],
        compiler_params=pltpu.CompilerParams(vmem_limit_bytes=8 * 1024 * 1024),
        cost_estimate=pl.CostEstimate(flops=0, bytes_accessed=8 * math.prod(shape), transcendentals=0),
    )(*[pltpu.with_memory_space_constraint(f, pltpu.HBM) for f in fields])
    return packed.reshape(count, 4 * (levels // count) * rows, cols)


def place_body(count, per, *refs):
    got, outs, sems = refs[0], refs[1:5], refs[5]
    copy_all([(got.at[d, :, f], outs[f].at[pl.ds(d * per, per)]) for d in range(count) for f in range(4)], sems)


def place(got, shape):
    count = got.shape[0]
    per = shape[0] // count
    return pl.pallas_call(
        functools.partial(place_body, count, per),
        in_specs=[pl.BlockSpec(memory_space=pltpu.VMEM)],
        out_specs=[pl.BlockSpec(memory_space=pl.ANY)] * 4,
        out_shape=[jax.ShapeDtypeStruct(shape, jnp.float32)] * 4,
        scratch_shapes=[pltpu.SemaphoreType.DMA((4 * count,))],
        compiler_params=pltpu.CompilerParams(vmem_limit_bytes=32 * 1024 * 1024),
        cost_estimate=pl.CostEstimate(flops=0, bytes_accessed=8 * got.size, transcendentals=0),
    )(got.reshape(count, per, 4, shape[1], shape[2]))


def lat_shift(x, amount, edge):
    size = x.shape[0]
    place = lax.broadcasted_iota(jnp.int32, x.shape, 0)
    at = size - 1 if amount < 0 else 0
    return jnp.where(place == at, edge, pltpu.roll(x, amount % size, 0))


def group_tendencies(level, first, size, span, rows, cols, dlon, dlat, place, geo_ref, got_ref, halo_refs, tend_ref, skip=0):
    start = pl.multiple_of(level * 4 * rows, 4 * rows)
    geo = geo_ref[pl.ds(pl.multiple_of(place * rows + first, 8), size), :]
    fs, fn, spin0, inv = geo[0:1, 3:4], geo[:, 4:5], geo[:, 5:6], geo[:, 6:7]
    to_east = (0.5 / dlon) * inv
    to_south, to_north = (0.5 / dlat) * (geo[:, 1:2] * inv), (0.5 / dlat) * (geo[:, 2:3] * inv)
    out_x, out_y = (-1.0 / dlon) * inv, (-1.0 / dlat) * inv
    wide = span * cols + 2 * LANES
    signs = (-1.0, -1.0, 1.0, 1.0)

    def mid(x):
        return x[:, LANES : LANES + span * cols]

    def east_of(x):
        return pltpu.roll(x, wide - 1, 1)

    def west_of(x):
        return pltpu.roll(x, 1, 1)

    def joined(parts):
        return parts[0] if len(parts) == 1 else jnp.concatenate(parts, axis=1)

    def edge_row(f, r, row, side, at_pole):
        if 0 <= row < rows:
            return got_ref[r, pl.ds(start + f * rows + row, 1), :]
        near = 0 if row < 0 else rows - 1
        across = got_ref[(r + SECTORS // 2) % SECTORS, pl.ds(start + f * rows + near, 1), :]
        per = got_ref.shape[1] // (4 * rows)
        at = pl.ds((r * per + level) * 4 + f, 1)
        halo = jnp.where(lax.rem(place, 2) == 1, halo_refs[side][at, :], halo_refs[1 - side][at, :])
        return jnp.where(at_pole, signs[f] * across, halo)

    for base in range(0, SECTORS, span):
        sectors = range(base, base + span)
        ext, south, north = [], [], []
        for f in range(4):
            part = pl.ds(pl.multiple_of(start + f * rows + first, 8), size)
            ext.append(
                jnp.concatenate(
                    [got_ref[(base - 1) % SECTORS, part, cols - LANES :]]
                    + [got_ref[r, part, :] for r in sectors]
                    + [got_ref[(base + span) % SECTORS, part, :LANES]],
                    axis=1,
                )
            )
            south.append(joined([edge_row(f, r, first - 1, 0, place == 0) for r in sectors]))
            north.append(joined([edge_row(f, r, first + size, 1, place == lax.axis_size("lat") - 1) for r in sectors]))
        ux, vx, px, hx = ext
        heat_x = px * hx
        energy_x = 0.5 * (ux * ux + vx * vx) + heat_x
        u, v, p, heat, energy = mid(ux), mid(vx), mid(px), mid(heat_x), mid(energy_x)

        spin = spin0 + (mid(east_of(vx)) - mid(west_of(vx))) * to_east
        spin -= to_north * lat_shift(u, -1, north[0]) - to_south * lat_shift(u, 1, south[0])
        edges = [0.5 * (q[0] * q[0] + q[1] * q[1]) + q[2] * q[3] for q in (south, north)]
        de_x = mid(east_of(energy_x)) - mid(west_of(energy_x))
        de_y = lat_shift(energy, -1, edges[1]) - lat_shift(energy, 1, edges[0])
        u_t = spin * v - de_x * to_east
        v_t = de_y * (-0.5 / dlat) - spin * u

        a = 0.5 * (ux + east_of(ux))
        ap, am = jnp.maximum(a, 0.0), jnp.minimum(a, 0.0)
        flow_x = ap * px + am * east_of(px)
        hot_x = ap * heat_x + am * east_of(heat_x)
        b = (0.5 * fn) * (v + lat_shift(v, -1, north[1]))
        bp, bm = jnp.maximum(b, 0.0), jnp.minimum(b, 0.0)
        flow_y = bp * p + bm * lat_shift(p, -1, north[2])
        hot_y = bp * heat + bm * lat_shift(heat, -1, north[2] * north[3])
        b0 = (0.5 * fs) * (south[1] + v[0:1, :])
        bp0, bm0 = jnp.maximum(b0, 0.0), jnp.minimum(b0, 0.0)
        flow_y0 = bp0 * south[2] + bm0 * p[0:1, :]
        hot_y0 = bp0 * (south[2] * south[3]) + bm0 * heat[0:1, :]
        p_t = (mid(flow_x) - mid(west_of(flow_x))) * out_x + (flow_y - lat_shift(flow_y, 1, flow_y0)) * out_y
        h_t = (mid(hot_x) - mid(west_of(hot_x))) * out_x + (hot_y - lat_shift(hot_y, 1, hot_y0)) * out_y
        for f, value in enumerate((u_t, v_t, p_t, h_t)):
            kept = rows - 2 * skip
            part = pl.ds(pl.multiple_of(level * 4 * kept + f * kept + first - skip, 8), size)
            for i, r in enumerate(sectors):
                tend_ref[r, part, :] = value[:, i * cols : (i + 1) * cols]


def butterfly(group, cols, tend_ref, parts_ref):
    rows_at = pl.ds(pl.multiple_of(group * 16, 16), 16)
    x = [tend_ref[b, rows_at, :] for b in range(SECTORS)]
    s = [x[b] + x[b + 4] for b in range(4)]
    d = [x[b] - x[b + 4] for b in range(4)]
    c = math.sqrt(0.5)
    even, odd = s[0] + s[2], s[1] + s[3]
    plus, minus = c * (d[1] + d[3]), c * (d[1] - d[3])
    parts = (even + odd, even - odd, d[0] + minus, -d[2] - plus, s[0] - s[2], s[3] - s[1], d[0] - minus, d[2] - plus)
    for i, part in enumerate(parts):
        start = (i // 2 * 4 + i % 2) * cols
        high, low = split(part)
        parts_ref[rows_at, start : start + cols] = high
        parts_ref[rows_at, start + 2 * cols : start + 3 * cols] = low


def truncate(total, cols, limit, ahead_ref, back_ref, parts_ref, wave_ref):
    lane = lax.broadcasted_iota(jnp.int32, (1, 2 * FULL_Q), 1)
    for r in range(4):
        at = slice(2 * r * cols, (2 * r + 2) * cols)
        both = slice(4 * r * cols, (4 * r + 4) * cols)
        high = slice(4 * r * cols, (4 * r + 2) * cols)
        spectrum = jnp.dot(parts_ref[:, both], ahead_ref[r, : 4 * cols], preferred_element_type=jnp.float32)
        spectrum += jnp.dot(parts_ref[:, high], ahead_ref[r, 4 * cols :], preferred_element_type=jnp.float32)
        if r == 0:
            k = SECTORS * lax.rem(lane, REAL_Q) + jnp.where(lane >= FULL_Q, 4, 0)
        else:
            k = jnp.abs(SECTORS * (lax.rem(lane, FULL_Q) - SHIFT_Q) + r)
        factor = jnp.where(k <= limit, jnp.where(k == 0, 1.0 / total, 2.0 / total), 0.0)
        high, low = split(spectrum * factor)
        both = jnp.concatenate([high, low, high], axis=1)
        wave_ref[:, at] = jnp.dot(both, back_ref[r], preferred_element_type=jnp.float32)


def update(level, rows, cols, step_size, listed, got_ref, tend_ref, wave_ref, out_ref):
    c = math.sqrt(0.5)
    high = 4 * rows
    for f in range(4):
        for j in range(0, rows, 8):
            at = pl.ds(pl.multiple_of(level * high + f * rows + j, 8), 8)
            w0, w4, a1, b1, a2, b2, a3, b3 = [wave_ref[at, i * cols : (i + 1) * cols] for i in range(SECTORS)]
            near, far = w0 + w4, w0 - w4
            even = (near + a2, far - b2, near - a2, far + b2)
            odd = (a1 + a3, c * ((a1 - b1) - (a3 + b3)), b3 - b1, c * ((a3 - b3) - (a1 + b1)))
            chosen = listed[j : j + 8, :]
            for b in range(SECTORS):
                smooth = even[b % 4] + odd[b % 4] if b < 4 else even[b % 4] - odd[b % 4]
                base = got_ref[b, at, :]
                if f == 3:
                    base = base * got_ref[b, pl.ds(pl.multiple_of(level * high + 2 * rows + j, 8), 8), :]
                out_ref[b, at, :] = base + step_size * jnp.where(chosen, smooth, tend_ref[b, at, :])


def edges_body(per, rows, got_ref, inner_ref, outer_ref, held_ref, sems):
    parts = range(4 * per)
    pairs = [(got_ref.at[:, pl.ds(q * rows, 8), :], held_ref.at[0, q]) for q in parts]
    pairs += [(got_ref.at[:, pl.ds((q + 1) * rows - 8, 8), :], held_ref.at[1, q]) for q in parts]
    copy_all(pairs, sems)
    odd = lax.rem(lax.axis_index("lat"), 2) == 1
    for r in range(SECTORS):
        for q in parts:
            at = r * 4 * per + q
            low, high = held_ref[0, q, r, 0:1, :], held_ref[1, q, r, 7:8, :]
            inner_ref[at : at + 1, :] = jnp.where(odd, low, high)
            outer_ref[at : at + 1, :] = jnp.where(odd, high, low)


def edge_rows(rows, got):
    count, height, cols = got.shape
    inside = pl.BlockSpec(memory_space=pltpu.VMEM)
    return pl.pallas_call(
        functools.partial(edges_body, height // (4 * rows), rows),
        in_specs=[pl.BlockSpec(memory_space=pltpu.HBM)],
        out_specs=[inside] * 2,
        out_shape=[jax.ShapeDtypeStruct((count * height // rows, cols), jnp.float32)] * 2,
        scratch_shapes=[
            pltpu.VMEM((2, height // rows, count, 8, cols), jnp.float32),
            pltpu.SemaphoreType.DMA((2 * height // rows,)),
        ],
        compiler_params=pltpu.CompilerParams(vmem_limit_bytes=8 * 1024 * 1024),
        cost_estimate=pl.CostEstimate(flops=0, bytes_accessed=16 * count * height // rows * cols, transcendentals=0),
    )(got)


def arrivals(per, high, far_ref, near_ref, sems):
    def one(level):
        at = pl.ds(pl.multiple_of(level * high, high), high)
        return pltpu.make_async_copy(far_ref.at[:, at, :], near_ref.at[:, at, :], sems.at[level])

    for level in range(per):
        one(level).start()
    return one


def inner_body(per, rows, cols, dlon, dlat, geo_ref, far_ref, tend_ref, got_ref, sems):
    place = lax.axis_index("lat")
    arrival = arrivals(per, 4 * rows, far_ref, got_ref, sems)

    @pl.loop(0, per)
    def _(level):
        arrival(level).wait()
        for first in range(8, rows - 8, 8):
            group_tendencies(level, first, 8, 2, rows, cols, dlon, dlat, place, geo_ref, got_ref, None, tend_ref, 8)


def inner_tendencies(rows, dlon, dlat, geo, got):
    inside = pl.BlockSpec(memory_space=pltpu.VMEM)
    return pl.pallas_call(
        functools.partial(inner_body, got.shape[1] // (4 * rows), rows, got.shape[2], dlon, dlat),
        in_specs=[inside, pl.BlockSpec(memory_space=pltpu.HBM)],
        out_specs=inside,
        scratch_shapes=[pltpu.VMEM(got.shape, jnp.float32), pltpu.SemaphoreType.DMA((got.shape[1] // (4 * rows),))],
        out_shape=jax.ShapeDtypeStruct((got.shape[0], got.shape[1] // rows * (rows - 16), got.shape[2]), jnp.float32),
        compiler_params=pltpu.CompilerParams(vmem_limit_bytes=12 * 1024 * 1024),
        cost_estimate=pl.CostEstimate(flops=40 * got.size, bytes_accessed=6 * got.size, transcendentals=0),
    )(geo, got)


def step_body(per, rows, cols, dlon, dlat, step_size, geo_ref, polar_ref, cutoff_ref, far_ref, tend_ref, inner_ref, outer_ref, *refs):
    ahead_ref, back_ref, out_ref, edge_ref, parts_ref, wave_ref, got_ref, sems = refs
    high = 4 * rows
    arrival = arrivals(per, high, far_ref, got_ref, sems)
    halos = (inner_ref, outer_ref)
    place = lax.axis_index("lat")
    total = rows * lax.axis_size("lat")
    edge = jnp.sum((polar_ref[...] < total // 2).astype(jnp.int32))
    own = place * rows + lax.broadcasted_iota(jnp.int32, (rows, 1), 0)
    listed = (own < edge) | (own >= total // 2 + edge)
    bands = LANES // rows
    cut = cutoff_ref[pl.ds(place // bands, 1), :]
    lane = lax.broadcasted_iota(jnp.int32, (rows, LANES), 1)
    mine = lane == lax.rem(place, bands) * rows + lax.broadcasted_iota(jnp.int32, (rows, LANES), 0)
    limit = jnp.sum(jnp.where(mine, cut, 0), axis=1, keepdims=True)
    limit = jnp.concatenate([limit] * (4 * per), axis=0)

    @pl.loop(0, per)
    def _(level):
        arrival(level).wait()
        for first in (0, rows - 8):
            group_tendencies(level, first, 8, 2, rows, cols, dlon, dlat, place, geo_ref, got_ref, halos, edge_ref)
        for f in range(4):
            part = pl.ds(pl.multiple_of(level * high + f * rows + 8, 8), rows - 16)
            kept = pl.ds(pl.multiple_of((level * 4 + f) * (rows - 16), 8), rows - 16)
            for r in range(SECTORS):
                edge_ref[r, part, :] = tend_ref[r, kept, :]

    @pl.loop(0, per * high // 16)
    def _(group):
        butterfly(group, cols, edge_ref, parts_ref)

    truncate(SECTORS * cols, cols, limit, ahead_ref, back_ref, parts_ref, wave_ref)

    @pl.loop(0, per)
    def _(level):
        update(level, rows, cols, step_size, listed, got_ref, edge_ref, wave_ref, out_ref)


def stepped(rows, dlon, dlat, step_size, geo, polar_rows, cutoffs, got, tend, inner, outer, tables):
    count, height, cols = got.shape
    inside = pl.BlockSpec(memory_space=pltpu.VMEM)
    full = count * cols
    return pl.pallas_call(
        functools.partial(step_body, height // (4 * rows), rows, cols, dlon, dlat, step_size),
        in_specs=[inside] * 3 + [pl.BlockSpec(memory_space=pltpu.HBM)] + [inside] * 5,
        out_specs=inside,
        out_shape=jax.ShapeDtypeStruct(got.shape, jnp.float32),
        scratch_shapes=[
            pltpu.VMEM(got.shape, jnp.float32),
            pltpu.VMEM((height, 2 * full), jnp.bfloat16),
            pltpu.VMEM((height, full), jnp.float32),
            pltpu.VMEM(got.shape, jnp.float32),
            pltpu.SemaphoreType.DMA((height // (4 * rows),)),
        ],
        compiler_params=pltpu.CompilerParams(vmem_limit_bytes=32 * 1024 * 1024),
        cost_estimate=pl.CostEstimate(flops=8 * 1024 * 1024 * height, bytes_accessed=24 * height * full, transcendentals=0),
    )(geo, polar_rows, cutoffs, got, tend, inner, outer, *tables)


def per_device(u_wind, v_wind, thickness, theta, polar_rows, cutoffs):
    levels, rows, cols = u_wind.shape
    lat_count = lax.axis_size("lat")
    count = lax.axis_size("lon")
    total_rows = rows * lat_count
    total_cols = cols * count
    dlon = 2.0 * math.pi / total_cols
    dlat = math.pi / total_rows
    step_size = 0.25 * dlon
    fields = (u_wind, v_wind, thickness, theta)
    per = levels // count

    got = lax.all_to_all(pack(count, fields), "lon", 0, 0, tiled=True)

    got = pltpu.with_memory_space_constraint(got, pltpu.HBM)
    inner, outer = edge_rows(rows, got)
    across = [(i, i + 1) for i in range(1, lat_count - 1, 2)]
    within = [(i, i + 1) for i in range(0, lat_count, 2)]
    outer = lax.ppermute(outer, "lat", across + [(j, i) for i, j in across])
    inner = lax.ppermute(inner, "lat", within + [(j, i) for i, j in within])

    geo = jnp.asarray(geometry(total_rows))
    cutoffs = cutoffs.reshape(total_rows // LANES, LANES)
    tables = fourier_tables(total_cols)
    tend = inner_tendencies(rows, dlon, dlat, geo, got)
    fresh = stepped(rows, dlon, dlat, step_size, geo, polar_rows.T, cutoffs, got, tend, inner, outer, tables)
    return tuple(place(lax.all_to_all(fresh, "lon", 0, 0, tiled=True), u_wind.shape))


def solution(mesh):
    field = P(None, "lat", "lon")
    return jax.shard_map(
        per_device,
        mesh=mesh,
        in_specs=(field, field, field, field, P(), P()),
        out_specs=(field, field, field, field),
        check_vma=False,
    )
```

```python
import functools
import math

import jax
import jax.numpy as jnp
import numpy as np
from jax import lax
from jax.experimental import pallas as pl
from jax.experimental.pallas import tpu as pltpu
from jax.sharding import PartitionSpec as P

OMEGA = 30.0
SECTORS = 8
REAL_Q = 64
FULL_Q = 128
SHIFT_Q = 52
LANES = 128


def geometry(total_rows):
    row = np.arange(-1, total_rows + 1)
    dist = np.maximum(np.minimum(row, total_rows - 1 - row), 0)
    cos_row = np.sin(np.pi * (dist + 0.5) / total_rows)
    face = np.arange(total_rows + 1)
    cos_face = np.sin(np.pi * np.minimum(face, total_rows - face) / total_rows)
    spin = -2.0 * OMEGA * np.cos(np.pi * (np.arange(total_rows) + 0.5) / total_rows)
    table = np.zeros((total_rows, 8))
    table[:, 0] = cos_row[1:-1]
    table[:, 1] = cos_row[:-2]
    table[:, 2] = cos_row[2:]
    table[:, 3] = cos_face[:-1]
    table[:, 4] = cos_face[1:]
    table[:, 5] = spin
    table[:, 6] = 1.0 / cos_row[1:-1]
    return table.astype(np.float32)


def split(x):
    high = x.astype(jnp.bfloat16)
    return high, (x - high.astype(jnp.float32)).astype(jnp.bfloat16)


def fourier_tables(total):
    cols = total // SECTORS
    column = np.arange(cols)

    def angle(wave):
        return (column[:, None] * wave[None, :] % total) * (2.0 * np.pi / total)

    real = []
    for r in (0, 4):
        theta = angle(SECTORS * np.arange(REAL_Q) + r)
        real.append(np.concatenate([np.cos(theta), -np.sin(theta)], axis=1))
    gap = np.zeros_like(real[0])
    tables = [np.block([[real[0], gap], [gap, real[1]]])]
    for r in (1, 2, 3):
        theta = angle(SECTORS * (np.arange(FULL_Q) - SHIFT_Q) + r)
        cos, sin = np.cos(theta), np.sin(theta)
        tables.append(np.block([[cos, -sin], [sin, cos]]))

    def halves(table):
        table = table.astype(np.float32)
        high = table.astype(jnp.bfloat16)
        return np.concatenate([high, high, (table - high.astype(np.float32)).astype(jnp.bfloat16)], axis=1)

    tables = np.stack(tables)
    return [jnp.asarray(halves(t)) for t in (tables, tables.transpose(0, 2, 1))]


def copy_all(pairs, sems):
    copies = [pltpu.make_async_copy(src, dst, sems.at[i]) for i, (src, dst) in enumerate(pairs)]
    for copy in copies:
        copy.start()
    for copy in copies:
        copy.wait()


def pack_body(count, per, *refs):
    fields, out, sems = refs[:4], refs[4], refs[5]
    copy_all([(fields[f].at[pl.ds(d * per, per)], out.at[d, :, f]) for d in range(count) for f in range(4)], sems)


def pack(count, fields):
    levels, rows, cols = fields[0].shape
    shape = (count, levels // count, 4, rows, cols)
    packed = pl.pallas_call(
        functools.partial(pack_body, count, levels // count),
        in_specs=[pl.BlockSpec(memory_space=pl.ANY)] * 4,
        out_specs=pl.BlockSpec(memory_space=pltpu.VMEM),
        out_shape=pltpu.VMEM(shape, jnp.float32),
        scratch_shapes=[pltpu.SemaphoreType.DMA((4 * count,))],
        compiler_params=pltpu.CompilerParams(vmem_limit_bytes=8 * 1024 * 1024),
        cost_estimate=pl.CostEstimate(flops=0, bytes_accessed=8 * math.prod(shape), transcendentals=0),
    )(*[pltpu.with_memory_space_constraint(f, pltpu.HBM) for f in fields])
    return packed.reshape(count, 4 * (levels // count) * rows, cols)


def place_body(count, per, *refs):
    got, outs, sems = refs[0], refs[1:5], refs[5]
    copy_all([(got.at[d, :, f], outs[f].at[pl.ds(d * per, per)]) for d in range(count) for f in range(4)], sems)


def place(got, shape):
    count = got.shape[0]
    per = shape[0] // count
    return pl.pallas_call(
        functools.partial(place_body, count, per),
        in_specs=[pl.BlockSpec(memory_space=pltpu.VMEM)],
        out_specs=[pl.BlockSpec(memory_space=pl.ANY)] * 4,
        out_shape=[jax.ShapeDtypeStruct(shape, jnp.float32)] * 4,
        scratch_shapes=[pltpu.SemaphoreType.DMA((4 * count,))],
        compiler_params=pltpu.CompilerParams(vmem_limit_bytes=32 * 1024 * 1024),
        cost_estimate=pl.CostEstimate(flops=0, bytes_accessed=8 * got.size, transcendentals=0),
    )(got.reshape(count, per, 4, shape[1], shape[2]))


def lat_shift(x, amount, edge):
    size = x.shape[0]
    place = lax.broadcasted_iota(jnp.int32, x.shape, 0)
    at = size - 1 if amount < 0 else 0
    return jnp.where(place == at, edge, pltpu.roll(x, amount % size, 0))


def group_tendencies(level, first, size, span, rows, cols, dlon, dlat, place, geo_ref, got_ref, halo_refs, tend_ref, skip=0):
    start = pl.multiple_of(level * 4 * rows, 4 * rows)
    geo = geo_ref[pl.ds(pl.multiple_of(place * rows + first, 8), size), :]
    fs, fn, spin0, inv = geo[0:1, 3:4], geo[:, 4:5], geo[:, 5:6], geo[:, 6:7]
    to_east = (0.5 / dlon) * inv
    to_south, to_north = (0.5 / dlat) * (geo[:, 1:2] * inv), (0.5 / dlat) * (geo[:, 2:3] * inv)
    out_x, out_y = (-1.0 / dlon) * inv, (-1.0 / dlat) * inv
    wide = span * cols + 2 * LANES
    signs = (-1.0, -1.0, 1.0, 1.0)

    def mid(x):
        return x[:, LANES : LANES + span * cols]

    def east_of(x):
        return pltpu.roll(x, wide - 1, 1)

    def west_of(x):
        return pltpu.roll(x, 1, 1)

    def joined(parts):
        return parts[0] if len(parts) == 1 else jnp.concatenate(parts, axis=1)

    def edge_row(f, r, row, side, at_pole):
        if 0 <= row < rows:
            return got_ref[r, pl.ds(start + f * rows + row, 1), :]
        near = 0 if row < 0 else rows - 1
        across = got_ref[(r + SECTORS // 2) % SECTORS, pl.ds(start + f * rows + near, 1), :]
        per = got_ref.shape[1] // (4 * rows)
        at = pl.ds((r * per + level) * 4 + f, 1)
        halo = jnp.where(lax.rem(place, 2) == 1, halo_refs[side][at, :], halo_refs[1 - side][at, :])
        return jnp.where(at_pole, signs[f] * across, halo)

    for base in range(0, SECTORS, span):
        sectors = range(base, base + span)
        ext, south, north = [], [], []
        for f in range(4):
            part = pl.ds(pl.multiple_of(start + f * rows + first, 8), size)
            ext.append(
                jnp.concatenate(
                    [got_ref[(base - 1) % SECTORS, part, cols - LANES :]]
                    + [got_ref[r, part, :] for r in sectors]
                    + [got_ref[(base + span) % SECTORS, part, :LANES]],
                    axis=1,
                )
            )
            south.append(joined([edge_row(f, r, first - 1, 0, place == 0) for r in sectors]))
            north.append(joined([edge_row(f, r, first + size, 1, place == lax.axis_size("lat") - 1) for r in sectors]))
        ux, vx, px, hx = ext
        heat_x = px * hx
        energy_x = 0.5 * (ux * ux + vx * vx) + heat_x
        u, v, p, heat, energy = mid(ux), mid(vx), mid(px), mid(heat_x), mid(energy_x)

        spin = spin0 + (mid(east_of(vx)) - mid(west_of(vx))) * to_east
        spin -= to_north * lat_shift(u, -1, north[0]) - to_south * lat_shift(u, 1, south[0])
        edges = [0.5 * (q[0] * q[0] + q[1] * q[1]) + q[2] * q[3] for q in (south, north)]
        de_x = mid(east_of(energy_x)) - mid(west_of(energy_x))
        de_y = lat_shift(energy, -1, edges[1]) - lat_shift(energy, 1, edges[0])
        u_t = spin * v - de_x * to_east
        v_t = de_y * (-0.5 / dlat) - spin * u

        a = 0.5 * (ux + east_of(ux))
        ap, am = jnp.maximum(a, 0.0), jnp.minimum(a, 0.0)
        flow_x = ap * px + am * east_of(px)
        hot_x = ap * heat_x + am * east_of(heat_x)
        b = (0.5 * fn) * (v + lat_shift(v, -1, north[1]))
        bp, bm = jnp.maximum(b, 0.0), jnp.minimum(b, 0.0)
        flow_y = bp * p + bm * lat_shift(p, -1, north[2])
        hot_y = bp * heat + bm * lat_shift(heat, -1, north[2] * north[3])
        b0 = (0.5 * fs) * (south[1] + v[0:1, :])
        bp0, bm0 = jnp.maximum(b0, 0.0), jnp.minimum(b0, 0.0)
        flow_y0 = bp0 * south[2] + bm0 * p[0:1, :]
        hot_y0 = bp0 * (south[2] * south[3]) + bm0 * heat[0:1, :]
        p_t = (mid(flow_x) - mid(west_of(flow_x))) * out_x + (flow_y - lat_shift(flow_y, 1, flow_y0)) * out_y
        h_t = (mid(hot_x) - mid(west_of(hot_x))) * out_x + (hot_y - lat_shift(hot_y, 1, hot_y0)) * out_y
        for f, value in enumerate((u_t, v_t, p_t, h_t)):
            kept = rows - 2 * skip
            part = pl.ds(pl.multiple_of(level * 4 * kept + f * kept + first - skip, 8), size)
            for i, r in enumerate(sectors):
                tend_ref[r, part, :] = value[:, i * cols : (i + 1) * cols]


def butterfly(part, side, rows, cols, edge_ref, inner_ref, parts_ref):
    rows_at = pl.ds(pl.multiple_of(part * rows + side * 16, 16), 16)
    edge_at = pl.ds(pl.multiple_of(part * rows + side * (rows - 8), 8), 8)
    inner_at = pl.ds(pl.multiple_of(part * (rows - 16) + side * 8, 8), 8)
    x = []
    for b in range(SECTORS):
        pair = [edge_ref[b, edge_at, :], inner_ref[b, inner_at, :]]
        x.append(jnp.concatenate(pair[::-1] if side else pair, axis=0))
    s = [x[b] + x[b + 4] for b in range(4)]
    d = [x[b] - x[b + 4] for b in range(4)]
    c = math.sqrt(0.5)
    even, odd = s[0] + s[2], s[1] + s[3]
    plus, minus = c * (d[1] + d[3]), c * (d[1] - d[3])
    parts = (even + odd, even - odd, d[0] + minus, -d[2] - plus, s[0] - s[2], s[3] - s[1], d[0] - minus, d[2] - plus)
    for i, part in enumerate(parts):
        start = (i // 2 * 4 + i % 2) * cols
        high, low = split(part)
        parts_ref[rows_at, start : start + cols] = high
        parts_ref[rows_at, start + 2 * cols : start + 3 * cols] = low


def truncate(total, cols, limit, ahead_ref, back_ref, parts_ref, wave_ref):
    lane = lax.broadcasted_iota(jnp.int32, (1, 2 * FULL_Q), 1)
    for r in range(4):
        at = slice(2 * r * cols, (2 * r + 2) * cols)
        both = slice(4 * r * cols, (4 * r + 4) * cols)
        high = slice(4 * r * cols, (4 * r + 2) * cols)
        spectrum = jnp.dot(parts_ref[:, both], ahead_ref[r, : 4 * cols], preferred_element_type=jnp.float32)
        spectrum += jnp.dot(parts_ref[:, high], ahead_ref[r, 4 * cols :], preferred_element_type=jnp.float32)
        if r == 0:
            k = SECTORS * lax.rem(lane, REAL_Q) + jnp.where(lane >= FULL_Q, 4, 0)
        else:
            k = jnp.abs(SECTORS * (lax.rem(lane, FULL_Q) - SHIFT_Q) + r)
        factor = jnp.where(k <= limit, jnp.where(k == 0, 1.0 / total, 2.0 / total), 0.0)
        high, low = split(spectrum * factor)
        both = jnp.concatenate([high, low, high], axis=1)
        wave_ref[:, at] = jnp.dot(both, back_ref[r], preferred_element_type=jnp.float32)


def update(level, rows, cols, step_size, listed, got_ref, edge_ref, inner_ref, wave_ref, out_ref):
    c = math.sqrt(0.5)
    high = 4 * rows
    for f in range(4):
        for j in range(0, rows, 8):
            at = pl.ds(pl.multiple_of(level * high + f * rows + j, 8), 8)
            w0, w4, a1, b1, a2, b2, a3, b3 = [wave_ref[at, i * cols : (i + 1) * cols] for i in range(SECTORS)]
            near, far = w0 + w4, w0 - w4
            even = (near + a2, far - b2, near - a2, far + b2)
            odd = (a1 + a3, c * ((a1 - b1) - (a3 + b3)), b3 - b1, c * ((a3 - b3) - (a1 + b1)))
            chosen = listed[j : j + 8, :]
            if 0 < j < rows - 8:
                tend_ref = inner_ref
                tend_at = pl.ds(pl.multiple_of((level * 4 + f) * (rows - 16) + j - 8, 8), 8)
            else:
                tend_ref, tend_at = edge_ref, at
            for b in range(SECTORS):
                smooth = even[b % 4] + odd[b % 4] if b < 4 else even[b % 4] - odd[b % 4]
                base = got_ref[b, at, :]
                if f == 3:
                    base = base * got_ref[b, pl.ds(pl.multiple_of(level * high + 2 * rows + j, 8), 8), :]
                out_ref[b, at, :] = base + step_size * jnp.where(chosen, smooth, tend_ref[b, tend_at, :])


def edges_body(per, rows, got_ref, inner_ref, outer_ref, held_ref, sems):
    parts = range(4 * per)
    pairs = [(got_ref.at[:, pl.ds(q * rows, 8), :], held_ref.at[0, q]) for q in parts]
    pairs += [(got_ref.at[:, pl.ds((q + 1) * rows - 8, 8), :], held_ref.at[1, q]) for q in parts]
    copy_all(pairs, sems)
    odd = lax.rem(lax.axis_index("lat"), 2) == 1
    for r in range(SECTORS):
        for q in parts:
            at = r * 4 * per + q
            low, high = held_ref[0, q, r, 0:1, :], held_ref[1, q, r, 7:8, :]
            inner_ref[at : at + 1, :] = jnp.where(odd, low, high)
            outer_ref[at : at + 1, :] = jnp.where(odd, high, low)


def edge_rows(rows, got):
    count, height, cols = got.shape
    inside = pl.BlockSpec(memory_space=pltpu.VMEM)
    return pl.pallas_call(
        functools.partial(edges_body, height // (4 * rows), rows),
        in_specs=[pl.BlockSpec(memory_space=pltpu.HBM)],
        out_specs=[inside] * 2,
        out_shape=[jax.ShapeDtypeStruct((count * height // rows, cols), jnp.float32)] * 2,
        scratch_shapes=[
            pltpu.VMEM((2, height // rows, count, 8, cols), jnp.float32),
            pltpu.SemaphoreType.DMA((2 * height // rows,)),
        ],
        compiler_params=pltpu.CompilerParams(vmem_limit_bytes=8 * 1024 * 1024),
        cost_estimate=pl.CostEstimate(flops=0, bytes_accessed=16 * count * height // rows * cols, transcendentals=0),
    )(got)


def arrivals(per, high, far_ref, near_ref, sems):
    def one(level):
        at = pl.ds(pl.multiple_of(level * high, high), high)
        return pltpu.make_async_copy(far_ref.at[:, at, :], near_ref.at[:, at, :], sems.at[level])

    for level in range(per):
        one(level).start()
    return one


def inner_body(per, rows, cols, dlon, dlat, geo_ref, far_ref, tend_ref, got_ref, sems):
    place = lax.axis_index("lat")
    arrival = arrivals(per, 4 * rows, far_ref, got_ref, sems)

    @pl.loop(0, per)
    def _(level):
        arrival(level).wait()
        for first in range(8, rows - 8, 8):
            group_tendencies(level, first, 8, 4, rows, cols, dlon, dlat, place, geo_ref, got_ref, None, tend_ref, 8)


def inner_tendencies(rows, dlon, dlat, geo, got):
    inside = pl.BlockSpec(memory_space=pltpu.VMEM)
    return pl.pallas_call(
        functools.partial(inner_body, got.shape[1] // (4 * rows), rows, got.shape[2], dlon, dlat),
        in_specs=[inside, pl.BlockSpec(memory_space=pltpu.HBM)],
        out_specs=inside,
        scratch_shapes=[pltpu.VMEM(got.shape, jnp.float32), pltpu.SemaphoreType.DMA((got.shape[1] // (4 * rows),))],
        out_shape=jax.ShapeDtypeStruct((got.shape[0], got.shape[1] // rows * (rows - 16), got.shape[2]), jnp.float32),
        compiler_params=pltpu.CompilerParams(vmem_limit_bytes=12 * 1024 * 1024),
        cost_estimate=pl.CostEstimate(flops=40 * got.size, bytes_accessed=6 * got.size, transcendentals=0),
    )(geo, got)


def step_body(per, rows, cols, dlon, dlat, step_size, geo_ref, polar_ref, cutoff_ref, far_ref, tend_ref, inner_ref, outer_ref, *refs):
    ahead_ref, back_ref, out_ref, edge_ref, parts_ref, wave_ref, got_ref, sems = refs
    high = 4 * rows
    arrival = arrivals(per, high, far_ref, got_ref, sems)
    halos = (inner_ref, outer_ref)
    place = lax.axis_index("lat")
    total = rows * lax.axis_size("lat")
    edge = jnp.sum((polar_ref[...] < total // 2).astype(jnp.int32))
    own = place * rows + lax.broadcasted_iota(jnp.int32, (rows, 1), 0)
    listed = (own < edge) | (own >= total // 2 + edge)
    bands = LANES // rows
    cut = cutoff_ref[pl.ds(place // bands, 1), :]
    lane = lax.broadcasted_iota(jnp.int32, (rows, LANES), 1)
    mine = lane == lax.rem(place, bands) * rows + lax.broadcasted_iota(jnp.int32, (rows, LANES), 0)
    limit = jnp.sum(jnp.where(mine, cut, 0), axis=1, keepdims=True)
    limit = jnp.concatenate([limit] * (4 * per), axis=0)

    @pl.loop(0, per)
    def _(level):
        arrival(level).wait()
        for first in (0, rows - 8):
            group_tendencies(level, first, 8, 4, rows, cols, dlon, dlat, place, geo_ref, got_ref, halos, edge_ref)

    @pl.loop(0, 4 * per)
    def _(part):
        for side in (0, 1):
            butterfly(part, side, rows, cols, edge_ref, tend_ref, parts_ref)

    truncate(SECTORS * cols, cols, limit, ahead_ref, back_ref, parts_ref, wave_ref)

    @pl.loop(0, per)
    def _(level):
        update(level, rows, cols, step_size, listed, got_ref, edge_ref, tend_ref, wave_ref, out_ref)


def stepped(rows, dlon, dlat, step_size, geo, polar_rows, cutoffs, got, tend, inner, outer, tables):
    count, height, cols = got.shape
    inside = pl.BlockSpec(memory_space=pltpu.VMEM)
    full = count * cols
    return pl.pallas_call(
        functools.partial(step_body, height // (4 * rows), rows, cols, dlon, dlat, step_size),
        in_specs=[inside] * 3 + [pl.BlockSpec(memory_space=pltpu.HBM)] + [inside] * 5,
        out_specs=inside,
        out_shape=jax.ShapeDtypeStruct(got.shape, jnp.float32),
        scratch_shapes=[
            pltpu.VMEM(got.shape, jnp.float32),
            pltpu.VMEM((height, 2 * full), jnp.bfloat16),
            pltpu.VMEM((height, full), jnp.float32),
            pltpu.VMEM(got.shape, jnp.float32),
            pltpu.SemaphoreType.DMA((height // (4 * rows),)),
        ],
        compiler_params=pltpu.CompilerParams(vmem_limit_bytes=32 * 1024 * 1024),
        cost_estimate=pl.CostEstimate(flops=8 * 1024 * 1024 * height, bytes_accessed=24 * height * full, transcendentals=0),
    )(geo, polar_rows, cutoffs, got, tend, inner, outer, *tables)


def per_device(u_wind, v_wind, thickness, theta, polar_rows, cutoffs):
    levels, rows, cols = u_wind.shape
    lat_count = lax.axis_size("lat")
    count = lax.axis_size("lon")
    total_rows = rows * lat_count
    total_cols = cols * count
    dlon = 2.0 * math.pi / total_cols
    dlat = math.pi / total_rows
    step_size = 0.25 * dlon
    fields = (u_wind, v_wind, thickness, theta)
    per = levels // count

    got = lax.all_to_all(pack(count, fields), "lon", 0, 0, tiled=True)

    got = pltpu.with_memory_space_constraint(got, pltpu.HBM)
    inner, outer = edge_rows(rows, got)
    across = [(i, i + 1) for i in range(1, lat_count - 1, 2)]
    within = [(i, i + 1) for i in range(0, lat_count, 2)]
    outer = lax.ppermute(outer, "lat", across + [(j, i) for i, j in across])
    inner = lax.ppermute(inner, "lat", within + [(j, i) for i, j in within])

    geo = jnp.asarray(geometry(total_rows))
    cutoffs = cutoffs.reshape(total_rows // LANES, LANES)
    tables = fourier_tables(total_cols)
    tend = inner_tendencies(rows, dlon, dlat, geo, got)
    fresh = stepped(rows, dlon, dlat, step_size, geo, polar_rows.T, cutoffs, got, tend, inner, outer, tables)
    return tuple(place(lax.all_to_all(fresh, "lon", 0, 0, tiled=True), u_wind.shape))


def solution(mesh):
    field = P(None, "lat", "lon")
    return jax.shard_map(
        per_device,
        mesh=mesh,
        in_specs=(field, field, field, field, P(), P()),
        out_specs=(field, field, field, field),
        check_vma=False,
    )
```
